128 devices in a mesh: dp: 8 (over x, y_lo), tensor: 16 (over z, y_hi, core).
Axes of the slice: x: 4, y: 4 (y_hi: 2, y_lo: 2; y = y_hi * 2 + y_lo), z: 4, core: 2. Of those that a mesh axis runs over, the one named last changes fastest.
Arguments:
- inputs: bfloat16 [8192, 9216], P(('dp', 'tensor')), may hold values from -8.5 to 8.5
- queries: bfloat16 [8192, 9216], P('dp', 'tensor'), may hold values from -24 to 24
- d_attn: bfloat16 [8192, 9216], P('dp', 'tensor'), may hold values from -6 to 6
- w_key: bfloat16 [9216, 1536], P(None, 'tensor'), may hold values from -0.0625 to 0.0625
- w_value: bfloat16 [9216, 1536], P(None, 'tensor'), may hold values from -0.0625 to 0.0625
Outputs:
- d_input: bfloat16 [8192, 9216], P(('dp', 'tensor'))
- d_queries: bfloat16 [8192, 9216], P('dp', 'tensor')
- grad_key: float32 [9216, 1536], P('dp', 'tensor')
- grad_value: float32 [9216, 1536], P('dp', 'tensor')
The draws below stay inside these ranges and needn't reach their ends.
All inputs are finite; a program needn't handle non-finite values.
Results may differ from the reference program's by a relative error of at most 0.02.
Values may be sent and summed in bfloat16 or wider, within the bound.
No kernel may reach another device: no remote copies, remote signals or barrier semaphores. Data moves between devices by JAX's collectives and lax.ppermute only.
A program may use at most 256 MiB of HBM per device.

```python
import jax
import jax.numpy as jnp
from jax import lax

D = 9216
HEAD = 192
QHEADS = 48
KVHEADS = 8
LEN = 1024
SEQS = 8
TOKENS = 8192
N_TENSOR = 16


def key_matrix(key):
    key = jax.random.fold_in(key, 12)
    return jnp.clip(jax.random.normal(key, (D, KVHEADS * HEAD), jnp.float32), -6.0, 6.0) * D ** (-0.5)


def draw_inputs(key, part):
    key = jax.random.fold_in(key, 13)
    first = jax.random.fold_in(key, 0)
    entries = jnp.clip(jax.random.normal(first, (TOKENS, D), jnp.float32), -6.0, 6.0)
    return entries.astype(jnp.bfloat16)


def draw_w_key(key, part):
    return key_matrix(key).astype(jnp.bfloat16)


def draw_queries(key, part):
    own = jax.random.fold_in(key, 14)
    base = jnp.clip(jax.random.normal(own, (TOKENS, QHEADS * HEAD), jnp.float32), -6.0, 6.0)
    return base.astype(jnp.bfloat16)


def levels(stream_key, extent, pieces, low, largest):
    def one(axis_at, shards_of):
        steps = jax.random.uniform(jax.random.fold_in(jax.random.fold_in(stream_key, 6), axis_at), (shards_of,), jnp.float32, low / len(pieces), largest / len(pieces))
        return jnp.repeat(jnp.exp(steps), extent[axis_at] // shards_of).reshape((-1,) + (1,) * (len(extent) - axis_at - 1))

    factor_of = one(*pieces[0])
    for cut in pieces[1:]:
        factor_of = factor_of * one(*cut)
    return factor_of


def scatter_about(stream_key, shape, width, reach, pieces=(), dtype=jnp.bfloat16):
    result = width * jax.random.normal(stream_key, shape, jnp.float32)
    if pieces:
        result = result * levels(stream_key, shape, pieces, -0.22, 0.18)
    return jnp.clip(result, -reach, reach).astype(dtype)


def setup_inputs(seed: int = 0) -> dict:
    key_list = jax.random.split(jax.random.key(seed), 6)
    inputs = draw_inputs(jax.random.fold_in(key_list[5], 71), 0)
    queries = draw_queries(jax.random.fold_in(key_list[5], 71), 0)
    d_attn = scatter_about(key_list[2], (TOKENS, QHEADS * HEAD), 1.0, 6.0, ((0, 8), (1, 16)))
    w_key = draw_w_key(jax.random.fold_in(key_list[5], 71), 0)
    w_value = scatter_about(key_list[4], (D, KVHEADS * HEAD), D ** -0.5, 0.0625, ((1, 16),))
    return {"inputs": inputs, "queries": queries, "d_attn": d_attn, "w_key": w_key, "w_value": w_value}


def rounded(array):
    return lax.optimization_barrier(array.astype(jnp.bfloat16)).astype(jnp.float32)


def reference(inputs, queries, d_attn, w_key, w_value):
    group_size = QHEADS // KVHEADS
    half_head = HEAD // 2
    score_scale = HEAD ** -0.5
    positions = jnp.arange(LEN)
    causal = positions[:, None] >= positions[None, :]
    input_parts = []
    query_parts = []
    grad_key = jnp.zeros((D, KVHEADS * HEAD), jnp.float32)
    grad_value = jnp.zeros((D, KVHEADS * HEAD), jnp.float32)
    for sequence in range(SEQS):
        seq_rows = inputs[sequence * LEN:(sequence + 1) * LEN]
        seq_grads = d_attn[sequence * LEN:(sequence + 1) * LEN].astype(jnp.float32).reshape(LEN, KVHEADS, group_size, HEAD)
        queries4 = queries[sequence * LEN:(sequence + 1) * LEN].astype(jnp.float32).reshape(LEN, KVHEADS, group_size, HEAD)
        key_rows = jnp.dot(seq_rows, w_key, preferred_element_type=jnp.float32).astype(jnp.bfloat16)
        value_rows = jnp.dot(seq_rows, w_value, preferred_element_type=jnp.float32).astype(jnp.bfloat16)
        keys3 = key_rows.astype(jnp.float32).reshape(LEN, KVHEADS, HEAD)
        values3 = value_rows.astype(jnp.float32).reshape(LEN, KVHEADS, HEAD)
        scores = jnp.einsum("qgjd,kgd->gjqk", queries4, keys3) * score_scale
        scores = jnp.where(causal, scores, -jnp.inf)
        row_max = jnp.max(scores, -1, keepdims=True)
        attention = jnp.exp(scores - row_max)
        attention = attention / jnp.sum(attention, -1, keepdims=True)
        d_probs = jnp.einsum("qgjd,kgd->gjqk", seq_grads, values3)
        row_total = jnp.sum(attention * d_probs, -1, keepdims=True)
        d_scores = rounded(attention * (d_probs - row_total) * score_scale)
        attention_low = rounded(attention)
        d_query = jnp.einsum("gjqk,kgd->qgjd", d_scores, keys3).astype(jnp.bfloat16).reshape(LEN, -1)
        d_key = jnp.einsum("gjqk,qgjd->kgd", d_scores, queries4).astype(jnp.bfloat16).reshape(LEN, -1)
        d_value = jnp.einsum("gjqk,qgjd->kgd", attention_low, seq_grads).astype(jnp.bfloat16).reshape(LEN, -1)
        query_parts.append(d_query)
        total = jnp.zeros((LEN, D), jnp.float32)
        for member in range(N_TENSOR):
            k_lo = member * half_head
            term = jnp.dot(d_key[:, k_lo:k_lo + half_head], w_key[:, k_lo:k_lo + half_head].T, preferred_element_type=jnp.float32)
            term = term + jnp.dot(d_value[:, k_lo:k_lo + half_head], w_value[:, k_lo:k_lo + half_head].T, preferred_element_type=jnp.float32)
            total = total + rounded(term)
        input_parts.append(total.astype(jnp.bfloat16))
        contract = (((0,), (0,)), ((), ()))
        grad_key = grad_key + rounded(lax.dot_general(seq_rows, d_key, contract, preferred_element_type=jnp.float32))
        grad_value = grad_value + rounded(lax.dot_general(seq_rows, d_value, contract, preferred_element_type=jnp.float32))
    return jnp.concatenate(input_parts, 0), jnp.concatenate(query_parts, 0), grad_key, grad_value
```

```python
import functools

import jax
import jax.numpy as jnp
from jax import lax
from jax.experimental import pallas as pl
from jax.experimental.pallas import tpu as pltpu
from jax.sharding import Mesh, PartitionSpec as P

HEAD = 192
HALF = 96
BLOCK = 64
BF = jnp.bfloat16
F32 = jnp.float32
REL = ((0, 0), (3, 0), (1, 0), (0, 1), (2, 0), (3, 1), (1, 1), (2, 1))
FLIP = (3, 5, 6, 0, 7, 1, 2, 4)


def ring(value, axis, step):
    return lax.ppermute(value, axis, [(i, (i + step) % 4) for i in range(4)])


def pair(value, axis):
    return lax.ppermute(value, axis, [(0, 1), (1, 0)])


def attn_kernel(tab, q_ref, g_ref, own_ref, oth_ref, dq_ref, down_ref, doth_ref, kt, vt, kn, dkt, dvt):
    core = tab[8]
    lo = pl.multiple_of(core * HALF, HALF)
    hi = pl.multiple_of(HALF - core * HALF, HALF)
    scale = HEAD ** -0.5
    for half, ref, a, b in ((0, own_ref, lo, hi), (1, oth_ref, hi, lo)):
        for jj in range(4):
            blk = jnp.concatenate([ref[tab[2 * jj]], ref[tab[2 * jj + 1]]], 0)
            t = blk.T
            col = slice(256 * jj + 128 * half, 256 * jj + 128 * half + 128)
            kt[pl.ds(a, HALF), col] = t[0:96]
            vt[pl.ds(a, HALF), col] = t[96:192]
            kt[pl.ds(b, HALF), col] = t[192:288]
            vt[pl.ds(b, HALF), col] = t[288:384]
    kn[...] = kt[...].T
    dkt[...] = jnp.zeros_like(dkt)
    dvt[...] = jnp.zeros_like(dvt)
    row = lax.broadcasted_iota(jnp.int32, (256, 256), 0)
    col = lax.broadcasted_iota(jnp.int32, (256, 256), 1)
    parity = jnp.where(col < 128, core, 1 - core)
    pos = ((col % 128) // 64) * 128 + parity * 64 + col % 64
    mask = row >= pos
    for i in range(4):
        width = 256 * (i + 1)
        rows = slice(256 * i, 256 * i + 256)
        dqs = []
        for j in range(3):
            q = q_ref[rows, HEAD * j:HEAD * (j + 1)]
            g = g_ref[rows, HEAD * j:HEAD * (j + 1)]
            s = jnp.dot(q, kt[:, :width], preferred_element_type=F32)
            last = jnp.where(mask, s[:, width - 256:], -jnp.inf)
            s = last if i == 0 else jnp.concatenate([s[:, :width - 256], last], 1)
            top = jnp.max(s, -1, keepdims=True)
            p = jnp.exp((s - top) * scale)
            inv = 1.0 / jnp.sum(p, -1, keepdims=True)
            dp = jnp.dot(g, vt[:, :width], preferred_element_type=F32)
            pn = p * inv
            total = jnp.sum(pn * dp, -1, keepdims=True)
            ds = (pn * ((dp - total) * scale)).astype(BF)
            low = pn.astype(BF)
            dqs.append(jnp.dot(ds, kn[:width, :], preferred_element_type=F32).astype(BF))
            dims = (((0,), (0,)), ((), ()))
            dkt[:, :width] += lax.dot_general(q, ds, dims, preferred_element_type=F32)
            dvt[:, :width] += lax.dot_general(g, low, dims, preferred_element_type=F32)
        dq_ref[rows, :] = jnp.concatenate(dqs, 1)
    for half, ref, a, b in ((0, down_ref, lo, hi), (1, doth_ref, hi, lo)):
        for jj in range(4):
            col = slice(256 * jj + 128 * half, 256 * jj + 128 * half + 128)
            t = jnp.concatenate(
                [dkt[pl.ds(a, HALF), col], dvt[pl.ds(a, HALF), col], dkt[pl.ds(b, HALF), col], dvt[pl.ds(b, HALF), col]], 0
            ).T
            ref[tab[2 * jj]] = t[:64].astype(ref.dtype)
            ref[tab[2 * jj + 1]] = t[64:].astype(ref.dtype)


def attention(table, queries, d_attn, own, oth):
    vm = pl.BlockSpec(memory_space=pltpu.VMEM)
    return pl.pallas_call(
        attn_kernel,
        in_specs=[pl.BlockSpec(memory_space=pltpu.SMEM), vm, vm, vm, vm],
        out_specs=[vm, vm, vm],
        out_shape=[
            jax.ShapeDtypeStruct(queries.shape, BF),
            jax.ShapeDtypeStruct((8, BLOCK, 2 * HEAD), F32),
            jax.ShapeDtypeStruct((8, BLOCK, 2 * HEAD), BF),
        ],
        scratch_shapes=[
            pltpu.VMEM((HEAD, 1024), BF),
            pltpu.VMEM((HEAD, 1024), BF),
            pltpu.VMEM((1024, HEAD), BF),
            pltpu.VMEM((HEAD, 1024), F32),
            pltpu.VMEM((HEAD, 1024), F32),
        ],
        compiler_params=pltpu.CompilerParams(vmem_limit_bytes=48 * 1024 * 1024),
        cost_estimate=pl.CostEstimate(flops=6 * 10**9, bytes_accessed=6 * 10**6, transcendentals=2 * 10**6),
        name="attention",
    )(table, queries, d_attn, own, oth)


def grad_kernel(place, dd_ref, x1_ref, x2_ref, keep_ref, send_ref, ddt):
    @pl.when(pl.program_id(0) == 0)
    def _():
        ddt[...] = dd_ref[...].T

    out = jnp.dot(ddt[:, :256], x1_ref[...], preferred_element_type=F32)
    out += jnp.dot(ddt[:, 256:], x2_ref[...], preferred_element_type=F32)
    out = out.astype(BF)
    keep_ref[0] = jnp.concatenate([out[0:192], out[384:576]], 0)
    send_ref[0] = jnp.concatenate([out[192:384], out[576:768]], 0)


def weight_grads(place, dd, x1, x2):
    width = x1.shape[1] // 4
    xs = pl.BlockSpec((256, width), lambda r, p: (0, (p[0] + r) % 4))
    out = pl.BlockSpec((1, 2 * HEAD, width), lambda r, p: (r, 0, 0))
    shape = jax.ShapeDtypeStruct((4, 2 * HEAD, width), BF)
    return pl.pallas_call(
        grad_kernel,
        grid_spec=pltpu.PrefetchScalarGridSpec(
            num_scalar_prefetch=1,
            grid=(4,),
            in_specs=[pl.BlockSpec((512, 4 * HEAD), lambda r, p: (0, 0)), xs, xs],
            out_specs=[out, out],
            scratch_shapes=[pltpu.VMEM((4 * HEAD, 512), BF)],
        ),
        out_shape=[shape, shape],
        compiler_params=pltpu.CompilerParams(vmem_limit_bytes=40 * 1024 * 1024),
        cost_estimate=pl.CostEstimate(flops=3624 * 10**6, bytes_accessed=13 * 10**6, transcendentals=0),
        name="weight_grads",
    )(place, dd, x1, x2)


def body(inputs, queries, d_attn, w_key, w_value):
    x, l, z, h, c = (lax.axis_index(name) for name in ("x", "l", "z", "h", "c"))
    width = inputs.shape[1] // 8

    def halves(array):
        parts = [array[:, width * i:width * (i + 1)] for i in range(8)]
        even = jnp.concatenate(parts[0::2], 1)
        odd = jnp.concatenate(parts[1::2], 1)
        return jnp.where(h == 0, even, odd), jnp.where(h == 0, odd, even)

    own, theirs = halves(inputs)
    q = pair(theirs, "h")
    a = ring(own, "z", 1)
    b = ring(own, "z", -1)
    wt = jnp.concatenate([w_key.T, w_value.T], 0)
    w_mine, w_theirs = halves(wt)
    w_partner = pair(w_theirs, "h")
    w_other = pair(w_mine, "c")
    w_partner_other = pair(w_partner, "c")
    o0 = ring(a[:32], "z", 1)
    o1 = ring(b[32:], "z", -1)
    qa = ring(q, "z", 1)
    qb = ring(q, "z", -1)
    qo0 = ring(qa[:32], "z", 1)
    qo1 = ring(qb[32:], "z", -1)
    w_all = jnp.concatenate([w_mine, w_other, w_partner, w_partner_other], 0)
    x1 = jnp.concatenate([own, a, b, q], 0)
    x2 = jnp.concatenate([o0, o1, qa, qb, qo0, qo1], 0)
    last = (((1,), (1,)), ((), ()))
    p1 = lax.dot_general(x1, w_all, last, preferred_element_type=F32)
    p2 = lax.dot_general(x2, w_all, last, preferred_element_type=F32)
    r1 = pair(p1[:, 2 * HEAD:].astype(BF), "h")
    r2 = pair(p2[:, 2 * HEAD:].astype(BF), "h")
    mine = jnp.concatenate([p1[:, :2 * HEAD], p2[:, :2 * HEAD]], 0)
    got = jnp.concatenate([r1, r2], 0).reshape(8, BLOCK, 2 * HEAD)
    got = jnp.concatenate([got[k:k + 1] for k in FLIP], 0)
    kv = (mine.reshape(8, BLOCK, 2 * HEAD) + got.astype(F32)).astype(BF)
    kv_other = pair(kv, "c")
    zz = jnp.arange(8, dtype=jnp.int32) // 2
    hh = jnp.arange(8, dtype=jnp.int32) % 2
    lookup = jnp.array([REL.index((k // 2, k % 2)) for k in range(8)], jnp.int32)
    table = jnp.concatenate([lookup[((zz - z) % 4) * 2 + (hh ^ h)], c[None].astype(jnp.int32)])
    d_query, d_own, d_oth = attention(table, queries, d_attn, kv, kv_other)
    d_oth = pair(d_oth, "c")
    dd = (d_own + d_oth.astype(F32)).astype(BF)
    dp = pair(dd, "h")
    dp = jnp.concatenate([dp[k:k + 1] for k in FLIP], 0)
    dd = jnp.concatenate([dd, dp], 2)

    def partial(first, second):
        return jnp.dot(
            jnp.concatenate([dd[first], dd[second]], 0), w_all, preferred_element_type=F32
        )

    ga = partial(7, 5).astype(BF)
    gb = partial(6, 4)
    gc = partial(2, 1)
    gd = partial(3, 0)
    up2 = ring(ga[:64], "z", 1)
    dn1 = ring(ga[64:], "z", -1)
    dn2 = ring(gb[64:].astype(BF), "z", -1)
    up1 = ring((gb[:64] + up2.astype(F32)).astype(BF), "z", 1)
    up0 = ring(gc[:64].astype(BF), "z", 1)
    dn0 = ring((gc[64:] + dn2.astype(F32)).astype(BF), "z", -1)
    cross = pair((gd[:64] + up1.astype(F32) + dn1.astype(F32)).astype(BF), "h")
    here = (gd[64:] + up0.astype(F32) + dn0.astype(F32)).astype(BF)

    def spread(even, odd):
        parts = []
        for k in range(4):
            parts += [even[:, width * k:width * (k + 1)], odd[:, width * k:width * (k + 1)]]
        return jnp.concatenate(parts, 1)

    d_input = jnp.where(h == 0, spread(here, cross), spread(cross, here))

    keep, send = weight_grads(x[None].astype(jnp.int32), dd.reshape(512, 4 * HEAD), x1, x2)
    got = pair(send, "c")
    blocks = [keep[r].astype(F32) + got[r].astype(F32) for r in range(4)]
    far = blocks[2].astype(BF)
    f0 = ring(far[:HEAD], "x", 1).astype(F32)
    f1 = ring(far[HEAD:], "x", -1).astype(F32)
    up = jnp.concatenate([blocks[1][:HEAD] + f0, blocks[1][HEAD:]], 0).astype(BF)
    down = jnp.concatenate([blocks[3][:HEAD], blocks[3][HEAD:] + f1], 0).astype(BF)
    up = ring(up, "x", 1)
    down = ring(down, "x", -1)
    total = blocks[0] + up.astype(F32) + down.astype(F32)
    same = l == h
    low = total.astype(BF)
    first = jnp.where(same, low[HEAD:], low[:HEAD])
    got1 = lax.ppermute(first, ("l", "h"), [(2, 0), (1, 3), (0, 1), (3, 2)])
    got2 = lax.ppermute(low[HEAD:], ("l", "h"), [(2, 1), (1, 2)])
    total = jnp.where(same, total[:HEAD], got2.astype(F32)) + got1.astype(F32)
    return d_input, d_query, total[:HALF].T, total[HALF:].T


def solution(mesh):
    fine = Mesh(mesh.devices.reshape(4, 2, 4, 2, 2), ("x", "l", "z", "h", "c"))
    dp, tensor = ("x", "l"), ("z", "h", "c")
    return jax.shard_map(
        body,
        mesh=fine,
        in_specs=(P(dp + tensor, None), P(dp, tensor), P(dp, tensor), P(None, tensor), P(None, tensor)),
        out_specs=(P(dp + tensor, None), P(dp, tensor), P(dp, tensor), P(dp, tensor)),
        check_vma=False,
    )
```

```python
import functools

import jax
import jax.numpy as jnp
from jax import lax
from jax.experimental import pallas as pl
from jax.experimental.pallas import tpu as pltpu
from jax.sharding import Mesh, PartitionSpec as P

HEAD = 192
HALF = 96
BLOCK = 64
ROWS = 256
BF = jnp.bfloat16
F32 = jnp.float32
VM = pl.BlockSpec(memory_space=pltpu.VMEM)
PLACE_X, PLACE_Z, PLACE_H, PLACE_C, PLACE_L = range(5)


def ring(value, axis, step):
    return lax.ppermute(value, axis, [(i, (i + step) % 4) for i in range(4)])


def pair(value, axis):
    return lax.ppermute(value, axis, [(0, 1), (1, 0)])


def after(value, *others):
    return lax.optimization_barrier((value, *others))[0]


def attn_kernel(at, q_ref, g_ref, own_ref, oth_ref, dq_ref, down_ref, doth_ref, kt, vt, kn, dkt, dvt):
    core, z, h = at[PLACE_C], at[PLACE_Z], at[PLACE_H]
    step = pl.program_id(0)
    lo = pl.multiple_of(core * HALF, HALF)
    hi = pl.multiple_of(HALF - core * HALF, HALF)
    scale = HEAD ** -0.5

    def place(chip):
        return ((chip // 2 + 4 - z) % 4) + 4 * ((chip % 2 + h) % 2)

    @pl.when(step == 0)
    def _():
        for half, ref, a, b in ((0, own_ref, lo, hi), (1, oth_ref, hi, lo)):
            for jj in range(4):
                blk = jnp.concatenate([ref[place(2 * jj)], ref[place(2 * jj + 1)]], 0)
                t = blk.T
                col = slice(256 * jj + 128 * half, 256 * jj + 128 * half + 128)
                kt[pl.ds(a, HALF), col] = t[0:96]
                vt[pl.ds(a, HALF), col] = t[96:192]
                kt[pl.ds(b, HALF), col] = t[192:288]
                vt[pl.ds(b, HALF), col] = t[288:384]
        kn[...] = kt[...].T
        dkt[...] = jnp.zeros_like(dkt)
        dvt[...] = jnp.zeros_like(dvt)

    row = lax.broadcasted_iota(jnp.int32, (ROWS, 256), 0)
    col = lax.broadcasted_iota(jnp.int32, (ROWS, 256), 1)
    parity = jnp.where(col < 128, core, 1 - core)
    pos = ((col % 128) // 64) * 128 + parity * 64 + col % 64
    mask = row >= pos

    def block(i):
        width = 256 * (i + 1)
        for j in range(3):
            qt = q_ref[HEAD * j:HEAD * (j + 1), :]
            gt = g_ref[HEAD * j:HEAD * (j + 1), :]
            s = jnp.dot(qt.T, kt[:, :width], preferred_element_type=F32)
            last = jnp.where(mask, s[:, width - 256:], -jnp.inf)
            s = last if i == 0 else jnp.concatenate([s[:, :width - 256], last], 1)
            top = jnp.max(s, -1, keepdims=True)
            p = jnp.exp((s - top) * scale)
            inv = 1.0 / jnp.sum(p, -1, keepdims=True)
            dp = jnp.dot(gt.T, vt[:, :width], preferred_element_type=F32)
            pn = p * inv
            total = jnp.sum(pn * dp, -1, keepdims=True)
            ds = (pn * ((dp - total) * scale)).astype(BF)
            low = pn.astype(BF)
            dq = jnp.dot(ds, kn[:width, :], preferred_element_type=F32).astype(BF)
            dq_ref[HEAD * j:HEAD * (j + 1), :] = dq.T
            dkt[:, :width] += jnp.dot(qt, ds, preferred_element_type=F32)
            dvt[:, :width] += jnp.dot(gt, low, preferred_element_type=F32)

    for i in range(4):
        pl.when(step == i)(functools.partial(block, i))

    @pl.when(step == 3)
    def _():
        for half, ref, a, b in ((0, down_ref, lo, hi), (1, doth_ref, hi, lo)):
            for jj in range(4):
                col = slice(256 * jj + 128 * half, 256 * jj + 128 * half + 128)
                t = jnp.concatenate(
                    [dkt[pl.ds(a, HALF), col], dvt[pl.ds(a, HALF), col], dkt[pl.ds(b, HALF), col], dvt[pl.ds(b, HALF), col]], 0
                ).T
                ref[place(2 * jj)] = t[:64].astype(ref.dtype)
                ref[place(2 * jj + 1)] = t[64:].astype(ref.dtype)


def attention(at, queries, d_attn, own, oth):
    rows = pl.BlockSpec((queries.shape[0], ROWS), lambda i, at: (0, i))
    whole = pl.BlockSpec((8, BLOCK, 2 * HEAD), lambda i, at: (0, 0, 0))
    return pl.pallas_call(
        attn_kernel,
        grid_spec=pltpu.PrefetchScalarGridSpec(
            num_scalar_prefetch=1,
            grid=(queries.shape[1] // ROWS,),
            in_specs=[rows, rows, whole, whole],
            out_specs=[rows, whole, whole],
            scratch_shapes=[
                pltpu.VMEM((HEAD, 1024), BF),
                pltpu.VMEM((HEAD, 1024), BF),
                pltpu.VMEM((1024, HEAD), BF),
                pltpu.VMEM((HEAD, 1024), F32),
                pltpu.VMEM((HEAD, 1024), F32),
            ],
        ),
        out_shape=[
            jax.ShapeDtypeStruct(queries.shape, BF),
            jax.ShapeDtypeStruct((8, BLOCK, 2 * HEAD), F32),
            jax.ShapeDtypeStruct((8, BLOCK, 2 * HEAD), BF),
        ],
        compiler_params=pltpu.CompilerParams(vmem_limit_bytes=28 * 1024 * 1024),
        cost_estimate=pl.CostEstimate(flops=8 * 10**9, bytes_accessed=6 * 10**6, transcendentals=2 * 10**6),
        name="attention",
    )(at, queries, d_attn, own, oth)


def local(kernel, out_shape, name, semaphores, *args):
    many = isinstance(out_shape, list)
    ins = pl.BlockSpec(memory_space=pl.ANY) if semaphores else VM
    return pl.pallas_call(
        kernel,
        in_specs=[pl.BlockSpec(memory_space=pltpu.SMEM)] + [ins] * (len(args) - 1),
        out_specs=[VM] * len(out_shape) if many else VM,
        out_shape=out_shape,
        scratch_shapes=[pltpu.SemaphoreType.DMA((semaphores,))] if semaphores else [],
        compiler_params=pltpu.CompilerParams(vmem_limit_bytes=24 * 1024 * 1024),
        cost_estimate=pl.CostEstimate(flops=1000, bytes_accessed=1000, transcendentals=0),
        name=name,
    )(*args)


def struct(rows, columns, dtype=BF):
    return jax.ShapeDtypeStruct((rows, columns), dtype)


def lanes(index, width):
    return pl.ds(pl.multiple_of(index * width, width), width)


def copies(pairs, sem):
    started = [pltpu.make_async_copy(a, b, sem.at[n]) for n, (a, b) in enumerate(pairs)]
    for copy in started:
        copy.start()
    for copy in started:
        copy.wait()


def pick_inputs(at, inputs, w_key, w_value):
    rows, width = inputs.shape[0], inputs.shape[1] // 8

    def kernel(at, in_ref, key_ref, value_ref, own_ref, theirs_ref, quarter_ref, sem):
        h, x = at[PLACE_H], at[PLACE_X]
        pairs = []
        for k in range(4):
            cols = slice(width * k, width * (k + 1))
            pairs.append((in_ref.at[:, lanes(2 * k + h, width)], own_ref.at[:, cols]))
            pairs.append((in_ref.at[:, lanes(2 * k + 1 - h, width)], theirs_ref.at[:, cols]))
        for n, ref in enumerate((key_ref, value_ref)):
            pairs.append((ref.at[:, lanes(2 * x + 1 - h, width)], quarter_ref.at[HALF * n:HALF * (n + 1), :]))
        copies(pairs, sem)

    out = [struct(rows, 4 * width)] * 2 + [struct(HEAD, width)]
    return local(kernel, out, "pick_inputs", 10, at, inputs, w_key, w_value)


def pick_weights(at, w_key, w_value):
    width = w_key.shape[1] // 8

    def kernel(at, key_ref, value_ref, mine_ref, sem):
        h = at[PLACE_H]
        pairs = []
        for n, ref in enumerate((key_ref, value_ref)):
            for k in range(4):
                out = mine_ref.at[HALF * n:HALF * (n + 1), width * k:width * (k + 1)]
                pairs.append((ref.at[:, lanes(2 * k + h, width)], out))
        copies(pairs, sem)

    return local(kernel, struct(HEAD, 4 * width), "pick_weights", 8, at, w_key, w_value)


def project_own(at, weights, pieces):
    rows = sum(p.shape[0] for p in pieces)
    width = pieces[0].shape[1] // 4

    def kernel(at, mine, other, *refs):
        xs, out_ref = refs[:-1], refs[-1]
        for k in range(4):
            cols = slice(width * k, width * (k + 1))
            x = jnp.concatenate([r[:, cols] for r in xs], 0)
            w = jnp.concatenate([mine[:, cols], other[:, cols]], 0)
            part = lax.dot_general(w, x, (((1,), (1,)), ((), ())), preferred_element_type=F32)
            total = part if k == 0 else total + part
        out_ref[...] = total.T

    return local(kernel, struct(rows, 2 * HEAD, F32), "project_own", 0, at, *weights, *pieces)


def project_partner(at, quarters, pieces):
    rows = sum(p.shape[0] for p in pieces)
    width = pieces[0].shape[1] // 4

    def kernel(at, *refs):
        w, xs, out_ref = refs[:8], refs[8:-1], refs[-1]
        for r in range(4):
            cols = lanes((at[PLACE_X] + r) % 4, width)
            x = jnp.concatenate([ref[:, cols] for ref in xs], 0)
            both = jnp.concatenate([w[r][...], w[4 + r][...]], 0)
            part = lax.dot_general(both, x, (((1,), (1,)), ((), ())), preferred_element_type=F32)
            total = part if r == 0 else total + part
        out_ref[...] = total.T.astype(BF)

    return local(kernel, struct(rows, 2 * HEAD), "project_partner", 0, at, *quarters, *pieces)


def weight_grads(at, dd, pieces, swapped, order):
    width = pieces[0].shape[1] // 4

    def kernel(at, dd_ref, *refs):
        xs, outs = refs[:-4], refs[-4:]
        ddt = jnp.concatenate([dd_ref[(k + 4 * swapped) % 8] for k in range(8)], 0).T
        for n, r in enumerate(order):
            cols = lanes((at[PLACE_X] + r) % 4, width)
            x = jnp.concatenate([ref[:, cols] for ref in xs], 0)
            out = jnp.dot(ddt, x, preferred_element_type=F32).astype(BF)
            outs[2 * (n // 2)][n % 2] = out[:HEAD]
            outs[2 * (n // 2) + 1][n % 2] = out[HEAD:]

    out = [jax.ShapeDtypeStruct((2, HEAD, width), BF)] * 4
    return local(kernel, out, "weight_grads", 0, at, dd, *pieces)


def finish(at, own, got_own, got_p, got_q):
    def kernel(at, own_ref, a_ref, b_ref, c_ref, key_ref, value_ref):
        same = at[PLACE_H] == at[PLACE_L]
        mine = own_ref[...] + a_ref[...].astype(F32)
        total = jnp.where(same, mine, b_ref[...].astype(F32) + c_ref[...].astype(F32))
        key_ref[...] = total[:HALF]
        value_ref[...] = total[HALF:]

    return local(kernel, [struct(HALF, own.shape[1], F32)] * 2, "finish", 0, at, own, got_own, got_p, got_q)


def join(at, own1, own2, got1, got2):
    mine = ((0, 0), (0, 1), (1, 0), (0, 2), (0, 3), (1, 1), (1, 2), (1, 3))
    theirs = ((0, 3), (1, 1), (1, 2), (1, 3), (0, 0), (0, 1), (1, 0), (0, 2))

    def kernel(at, own1_ref, own2_ref, got1_ref, got2_ref, out_ref):
        own, got = (own1_ref, own2_ref), (got1_ref, got2_ref)
        for k in range(8):
            (n, i), (m, j) = mine[k], theirs[k]
            a = own[n][BLOCK * i:BLOCK * (i + 1), :]
            b = got[m][BLOCK * j:BLOCK * (j + 1), :]
            out_ref[k] = (a + b.astype(F32)).astype(BF)

    out = jax.ShapeDtypeStruct((8, BLOCK, 2 * HEAD), BF)
    return local(kernel, out, "join", 0, at, own1, own2, got1, got2)


def input_grads(at, dd, dp, weights, quarters, first, second, types):
    width = weights[0].shape[1] // 4

    def kernel(at, dd_ref, dp_ref, w0, w1, *refs):
        w, (out1_ref, out2_ref) = refs[:8], refs[8:]
        own = jnp.concatenate([dd_ref[first], dd_ref[second]], 0)
        other = jnp.concatenate([dp_ref[(first + 4) % 8], dp_ref[(second + 4) % 8]], 0)
        for r in range(4):
            cols = lanes((at[PLACE_X] + r) % 4, width)
            out = jnp.dot(own, jnp.concatenate([w0[:, cols], w1[:, cols]], 0), preferred_element_type=F32)
            out += jnp.dot(other, jnp.concatenate([w[r][...], w[4 + r][...]], 0), preferred_element_type=F32)
            out1_ref[:, cols] = out[:BLOCK].astype(out1_ref.dtype)
            out2_ref[:, cols] = out[BLOCK:].astype(out2_ref.dtype)

    out = [struct(BLOCK, 4 * width, t) for t in types]
    return local(kernel, out, "input_grads", 0, at, dd, dp, *weights, *quarters)


def spread(at, here, up, down, cross):
    rows, width = here.shape[0], here.shape[1] // 4

    def kernel(at, here_ref, up_ref, down_ref, cross_ref, out_ref):
        h = at[PLACE_H]
        for k in range(4):
            cols = slice(width * k, width * (k + 1))
            total = here_ref[:, cols] + up_ref[:, cols].astype(F32) + down_ref[:, cols].astype(F32)
            out_ref[:, lanes(2 * k + h, width)] = total.astype(BF)
            out_ref[:, lanes(2 * k + 1 - h, width)] = cross_ref[:, cols]

    return local(kernel, struct(rows, 8 * width), "spread", 0, at, here, up, down, cross)


def body(inputs, queries, d_attn, w_key, w_value):
    x, l, z, h, c = (lax.axis_index(name) for name in ("x", "l", "z", "h", "c"))
    at = jnp.stack([x, z, h, c, l]).astype(jnp.int32)

    own, theirs, quarter = pick_inputs(at, inputs, w_key.T, w_value.T)
    q = pair(theirs, "h")
    a = ring(own, "z", 1)
    b = ring(own, "z", -1)
    wq = pair(quarter, "h")
    w_mine = pick_weights(at, after(w_key, own).T, w_value.T)
    w_other = pair(w_mine, "c")
    o0 = ring(a[:32], "z", 1)
    o1 = ring(b[32:], "z", -1)
    q = after(q, o0, o1)
    qa = ring(q, "z", 1)
    qb = ring(q, "z", -1)
    quarters = [wq, ring(wq, "x", -1), ring(wq, "x", 2), ring(wq, "x", 1)]
    quarters += [pair(w, "c") for w in quarters]
    qo0 = ring(qa[:32], "z", 1)
    qo1 = ring(qb[32:], "z", -1)
    group1 = (own, b, a, q)
    group2 = (o0, o1, qb, qo0, qo1, qa)
    got1 = pair(project_partner(at, quarters, group1), "h")
    send2 = project_partner(at, quarters, group2)
    got2 = pair(send2, "h")
    own1 = project_own(at, (w_mine, w_other), (after(own, send2),) + group1[1:])
    own2 = project_own(at, (w_mine, w_other), (after(o0, send2),) + group2[1:])
    kv = join(at, own1, own2, got1, got2)
    d_query, d_own, d_oth = attention(at, queries.T, d_attn.T, kv, pair(kv, "c"))
    d_oth = pair(d_oth, "c")
    dd = (d_own + d_oth.astype(F32)).astype(BF)
    dp = pair(dd, "h")

    pieces = (own, b, o0, o1, a, q, qb, qo0, qo1, qa)
    weights = (w_mine, w_other)

    def add(first, second):
        return (first + second.astype(F32)).astype(BF)

    def reduced(dd, swapped, order):
        keep1, send1, keep2, send2 = weight_grads(at, dd, pieces, swapped, order)
        got1 = pair(send1, "c")
        got2 = pair(send2, "c")
        sums = {}
        for keep, got, part in ((keep1, got1, order[:2]), (keep2, got2, order[2:])):
            for n, r in enumerate(part):
                sums[r] = keep[n].astype(F32) + got[n].astype(F32)
        return sums

    so = reduced(dd, False, (2, 3, 1, 0))
    far_o, dn_o = so[2].astype(BF), so[3].astype(BF)
    dp = after(dp, far_o, dn_o)
    far_o = ring(far_o, "x", 1)
    dn_o = ring(dn_o, "x", -1)
    t2, t1 = input_grads(at, dd, dp, weights, quarters, 6, 7, (BF, BF))
    up2 = ring(t2, "z", 1)
    dn1 = ring(t1, "z", -1)
    sp = reduced(after(dp, t1), True, (2, 1, 3, 0))
    far_p, up_p = sp[2].astype(BF), sp[1].astype(BF)
    ddb = after(dd, far_p, up_p, far_o, dn_o)
    far_p = ring(far_p, "x", -1)
    up_o = ring(add(so[1], far_o), "x", 1)
    u1, t2 = input_grads(at, ddb, dp, weights, quarters, 5, 2, (F32, BF))
    dn2 = ring(t2, "z", -1)
    ddc = after(ddb, up2, dn1)
    up1 = ring(add(u1, up2), "z", 1)
    u0, d0 = input_grads(at, ddc, dp, weights, quarters, 1, 3, (BF, F32))
    cr, here = input_grads(at, ddc, dp, weights, quarters, 4, 0, (F32, F32))
    up_p = ring(up_p, "x", 1)
    dn_p = ring(add(sp[3], far_p), "x", -1)
    up0 = ring(u0, "z", 1)
    dn0 = ring(add(d0, dn2), "z", -1)
    total_o = so[0] + up_o.astype(F32) + dn_o.astype(F32)
    fin_o = lax.ppermute(total_o.astype(BF), ("l", "h"), [(2, 0), (1, 3)])
    cross = pair(add(cr + up1.astype(F32), dn1), "h")
    total_p = add(sp[0] + up_p.astype(F32), dn_p)
    fin_p = lax.ppermute(total_p, ("l", "h"), [(0, 1), (3, 2)])
    fin_q = lax.ppermute(total_p, ("l", "h"), [(2, 1), (1, 2)])
    d_input = spread(at, here, up0, dn0, cross)
    g_key, g_value = finish(at, total_o, fin_o, fin_p, fin_q)
    return d_input, d_query.T, g_key.T, g_value.T


def solution(mesh):
    fine = Mesh(mesh.devices.reshape(4, 2, 4, 2, 2), ("x", "l", "z", "h", "c"))
    dp, tensor = ("x", "l"), ("z", "h", "c")
    return jax.shard_map(
        body,
        mesh=fine,
        in_specs=(P(dp + tensor, None), P(dp, tensor), P(dp, tensor), P(None, tensor), P(None, tensor)),
        out_specs=(P(dp + tensor, None), P(dp, tensor), P(dp, tensor), P(dp, tensor)),
        check_vma=False,
    )
```

```python
import functools

import jax
import jax.numpy as jnp
from jax import lax
from jax.experimental import pallas as pl
from jax.experimental.pallas import tpu as pltpu
from jax.sharding import Mesh, PartitionSpec as P

HEAD = 192
HALF = 96
BLOCK = 64
ROWS = 256
BF = jnp.bfloat16
F32 = jnp.float32
VM = pl.BlockSpec(memory_space=pltpu.VMEM)
PLACE_X, PLACE_Z, PLACE_H, PLACE_C, PLACE_L = range(5)


def ring(value, axis, step):
    return lax.ppermute(value, axis, [(i, (i + step) % 4) for i in range(4)])


def pair(value, axis):
    return lax.ppermute(value, axis, [(0, 1), (1, 0)])


def after(value, *others):
    return lax.optimization_barrier((value, *others))[0]


def attn_kernel(at, q_ref, g_ref, own_ref, oth_ref, dq_ref, own_out, mine_out, send_out, kt, vt, kn, dkt, dvt):
    core, z, h = at[PLACE_C], at[PLACE_Z], at[PLACE_H]
    step = pl.program_id(0)
    lo = pl.multiple_of(core * HALF, HALF)
    hi = pl.multiple_of(HALF - core * HALF, HALF)
    scale = HEAD ** -0.5

    def place(chip):
        return ((chip // 2 + 4 - z) % 4) + 4 * ((chip % 2 + h) % 2)

    @pl.when(step == 0)
    def _():
        for half, ref, a, b in ((0, own_ref, lo, hi), (1, oth_ref, hi, lo)):
            for jj in range(4):
                blk = jnp.concatenate([ref[place(2 * jj)], ref[place(2 * jj + 1)]], 0)
                t = blk.T
                col = slice(256 * jj + 128 * half, 256 * jj + 128 * half + 128)
                kt[pl.ds(a, HALF), col] = t[0:96]
                vt[pl.ds(a, HALF), col] = t[96:192]
                kt[pl.ds(b, HALF), col] = t[192:288]
                vt[pl.ds(b, HALF), col] = t[288:384]
        kn[...] = kt[...].T
        dkt[...] = jnp.zeros_like(dkt)
        dvt[...] = jnp.zeros_like(dvt)

    row = lax.broadcasted_iota(jnp.int32, (ROWS, 256), 0)
    col = lax.broadcasted_iota(jnp.int32, (ROWS, 256), 1)
    parity = jnp.where(col < 128, core, 1 - core)
    pos = ((col % 128) // 64) * 128 + parity * 64 + col % 64
    mask = row >= pos

    def block(i):
        width = 256 * (i + 1)
        for j in range(3):
            qt = q_ref[HEAD * j:HEAD * (j + 1), :]
            gt = g_ref[HEAD * j:HEAD * (j + 1), :]
            s = jnp.dot(qt.T, kt[:, :width], preferred_element_type=F32)
            last = jnp.where(mask, s[:, width - 256:], -jnp.inf)
            s = last if i == 0 else jnp.concatenate([s[:, :width - 256], last], 1)
            top = jnp.max(s, -1, keepdims=True)
            p = jnp.exp((s - top) * scale)
            inv = 1.0 / jnp.sum(p, -1, keepdims=True)
            dp = jnp.dot(gt.T, vt[:, :width], preferred_element_type=F32)
            pn = p * inv
            total = jnp.sum(pn * dp, -1, keepdims=True)
            ds = (pn * ((dp - total) * scale)).astype(BF)
            low = pn.astype(BF)
            dq = jnp.dot(ds, kn[:width, :], preferred_element_type=F32).astype(BF)
            dq_ref[HEAD * j:HEAD * (j + 1), :] = dq.T
            dkt[:, :width] += jnp.dot(qt, ds, preferred_element_type=F32)
            dvt[:, :width] += jnp.dot(gt, low, preferred_element_type=F32)

    for i in range(4):
        pl.when(step == i)(functools.partial(block, i))

    @pl.when(step == 3)
    def _():
        for half, a, b in ((0, lo, hi), (1, hi, lo)):
            for jj in range(4):
                col = slice(256 * jj + 128 * half, 256 * jj + 128 * half + 128)
                t = jnp.concatenate(
                    [dkt[pl.ds(a, HALF), col], dvt[pl.ds(a, HALF), col], dkt[pl.ds(b, HALF), col], dvt[pl.ds(b, HALF), col]], 0
                ).T
                for n in range(2):
                    to, part = place(2 * jj + n), t[64 * n:64 * (n + 1)]
                    if half == 0:
                        own_out[to] = part
                        send_out[to, :, 2 * HEAD:] = part[:, HEAD:].astype(BF)
                    else:
                        send_out[to, :, :2 * HEAD] = part.astype(BF)
                        mine_out[to] = part[:, HEAD:]


def attention(at, queries, d_attn, own, oth):
    rows = pl.BlockSpec((queries.shape[0], ROWS), lambda i, at: (0, i))

    def spec(columns):
        return pl.BlockSpec((8, BLOCK, columns), lambda i, at: (0, 0, 0))

    whole = spec(2 * HEAD)
    return pl.pallas_call(
        attn_kernel,
        grid_spec=pltpu.PrefetchScalarGridSpec(
            num_scalar_prefetch=1,
            grid=(queries.shape[1] // ROWS,),
            in_specs=[rows, rows, whole, whole],
            out_specs=[rows, whole, spec(HEAD), spec(3 * HEAD)],
            scratch_shapes=[
                pltpu.VMEM((HEAD, 1024), BF),
                pltpu.VMEM((HEAD, 1024), BF),
                pltpu.VMEM((1024, HEAD), BF),
                pltpu.VMEM((HEAD, 1024), F32),
                pltpu.VMEM((HEAD, 1024), F32),
            ],
        ),
        out_shape=[
            jax.ShapeDtypeStruct(queries.shape, BF),
            jax.ShapeDtypeStruct((8, BLOCK, 2 * HEAD), F32),
            jax.ShapeDtypeStruct((8, BLOCK, HEAD), F32),
            jax.ShapeDtypeStruct((8, BLOCK, 3 * HEAD), BF),
        ],
        compiler_params=pltpu.CompilerParams(vmem_limit_bytes=28 * 1024 * 1024),
        cost_estimate=pl.CostEstimate(flops=8 * 10**9, bytes_accessed=6 * 10**6, transcendentals=2 * 10**6),
        name="attention",
    )(at, queries, d_attn, own, oth)


def local(kernel, out_shape, name, semaphores, *args):
    many = isinstance(out_shape, list)
    ins = pl.BlockSpec(memory_space=pl.ANY) if semaphores else VM
    return pl.pallas_call(
        kernel,
        in_specs=[pl.BlockSpec(memory_space=pltpu.SMEM)] + [ins] * (len(args) - 1),
        out_specs=[VM] * len(out_shape) if many else VM,
        out_shape=out_shape,
        scratch_shapes=[pltpu.SemaphoreType.DMA((semaphores,))] if semaphores else [],
        compiler_params=pltpu.CompilerParams(vmem_limit_bytes=24 * 1024 * 1024),
        cost_estimate=pl.CostEstimate(flops=1000, bytes_accessed=1000, transcendentals=0),
        name=name,
    )(*args)


def struct(rows, columns, dtype=BF):
    return jax.ShapeDtypeStruct((rows, columns), dtype)


def lanes(index, width):
    return pl.ds(pl.multiple_of(index * width, width), width)


def copies(pairs, sem):
    started = [pltpu.make_async_copy(a, b, sem.at[n]) for n, (a, b) in enumerate(pairs)]
    for copy in started:
        copy.start()
    for copy in started:
        copy.wait()


def pick_inputs(at, inputs):
    rows, width = inputs.shape[0], inputs.shape[1] // 8

    def kernel(at, in_ref, own_ref, theirs_ref):
        h = at[PLACE_H]
        for k in range(4):
            cols = slice(width * k, width * (k + 1))
            theirs_ref[:, cols] = in_ref[:, lanes(2 * k + 1 - h, width)]
            own_ref[:, cols] = in_ref[:, lanes(2 * k + h, width)]

    return local(kernel, [struct(rows, 4 * width)] * 2, "pick_inputs", 0, at, inputs)


def pick_weights(at, w_key, w_value):
    width = w_key.shape[1] // 8

    def kernel(at, key_ref, value_ref, quarter_ref, mine_ref):
        h, x = at[PLACE_H], at[PLACE_X]
        for n, ref in enumerate((key_ref, value_ref)):
            rows = slice(HALF * n, HALF * (n + 1))
            quarter_ref[rows, :] = ref[:, lanes(2 * x + 1 - h, width)]
            for k in range(4):
                mine_ref[rows, width * k:width * (k + 1)] = ref[:, lanes(2 * k + h, width)]

    out = [struct(HEAD, width), struct(HEAD, 4 * width)]
    return local(kernel, out, "pick_weights", 0, at, w_key, w_value)


def project_own(at, weights, pieces):
    rows = sum(p.shape[0] for p in pieces)
    width = pieces[0].shape[1] // 4

    def kernel(at, mine, other, *refs):
        xs, out_ref = refs[:-1], refs[-1]
        for k in range(4):
            cols = slice(width * k, width * (k + 1))
            x = jnp.concatenate([r[:, cols] for r in xs], 0)
            w = jnp.concatenate([mine[:, cols], other[:, cols]], 0)
            part = lax.dot_general(w, x, (((1,), (1,)), ((), ())), preferred_element_type=F32)
            total = part if k == 0 else total + part
        out_ref[...] = total.T

    return local(kernel, struct(rows, 2 * HEAD, F32), "project_own", 0, at, *weights, *pieces)


def project_partner(at, quarters, pieces):
    rows = sum(p.shape[0] for p in pieces)
    width = pieces[0].shape[1] // 4

    def kernel(at, *refs):
        w, xs, out_ref = refs[:8], refs[8:-1], refs[-1]
        for r in range(4):
            cols = lanes((at[PLACE_X] + r) % 4, width)
            x = jnp.concatenate([ref[:, cols] for ref in xs], 0)
            both = jnp.concatenate([w[r][...], w[4 + r][...]], 0)
            part = lax.dot_general(both, x, (((1,), (1,)), ((), ())), preferred_element_type=F32)
            total = part if r == 0 else total + part
        out_ref[...] = total.T.astype(BF)

    return local(kernel, struct(rows, 2 * HEAD), "project_partner", 0, at, *quarters, *pieces)


def merge(at, own, mine, got):
    def kernel(at, own_ref, mine_ref, got_ref, dd_ref, other_ref):
        for k in range(8):
            dd_ref[k] = (own_ref[k] + got_ref[k, :, :2 * HEAD].astype(F32)).astype(BF)
            other_ref[k] = (mine_ref[k] + got_ref[k, :, 2 * HEAD:].astype(F32)).astype(BF)

    out = [jax.ShapeDtypeStruct((8, BLOCK, n * HEAD), BF) for n in (2, 1)]
    return local(kernel, out, "merge", 0, at, own, mine, got)


def stack(at, groups, name):
    rows = [sum(p.shape[0] for p in g) for g in groups]
    width = groups[0][0].shape[1]
    count = [len(g) for g in groups]

    def kernel(at, *refs):
        ins, outs = refs[:sum(count)], refs[sum(count):]
        n = 0
        for out, many in zip(outs, count):
            row = 0
            for ref in ins[n:n + many]:
                out[row:row + ref.shape[0], :] = ref[...]
                row += ref.shape[0]
            n += many

    return local(kernel, [struct(r, width) for r in rows], name, 0, at, *[p for g in groups for p in g])


def weight_grads(at, dd, other, own_x, other_x, swapped, order):
    width = own_x.shape[1] // 4

    def kernel(at, dd_ref, other_ref, x_ref, ox_ref, *outs):
        def turned(ref):
            return jnp.concatenate([ref[(k + 4 * swapped) % 8][:, :HEAD] for k in range(8)], 0).T

        a, b = turned(dd_ref), turned(other_ref)
        for n, r in enumerate(order):
            cols = lanes((at[PLACE_X] + r) % 4, width)
            out = jnp.dot(a, x_ref[:, cols], preferred_element_type=F32)
            out += jnp.dot(b, ox_ref[:, cols], preferred_element_type=F32)
            outs[n][...] = out.astype(BF)

    return local(kernel, [struct(HEAD, width)] * 4, "weight_grads", 0, at, dd, other, own_x, other_x)


def finish(at, own, got_own, got_p, got_q):
    def kernel(at, own_ref, a_ref, b_ref, c_ref, key_ref, value_ref):
        same = at[PLACE_H] == at[PLACE_L]
        mine = own_ref[...].astype(F32) + a_ref[...].astype(F32)
        total = jnp.where(same, mine, b_ref[...].astype(F32) + c_ref[...].astype(F32))
        key_ref[...] = total[:HALF]
        value_ref[...] = total[HALF:]

    return local(kernel, [struct(HALF, own.shape[1], F32)] * 2, "finish", 0, at, own, got_own, got_p, got_q)


def join(at, own1, own2, got1, got2):
    mine = ((0, 0), (0, 1), (1, 0), (0, 2), (0, 3), (1, 1), (1, 2), (1, 3))
    theirs = ((0, 3), (1, 1), (1, 2), (1, 3), (0, 0), (0, 1), (1, 0), (0, 2))

    def kernel(at, own1_ref, own2_ref, got1_ref, got2_ref, out_ref):
        own, got = (own1_ref, own2_ref), (got1_ref, got2_ref)
        for k in range(8):
            (n, i), (m, j) = mine[k], theirs[k]
            a = own[n][BLOCK * i:BLOCK * (i + 1), :]
            b = got[m][BLOCK * j:BLOCK * (j + 1), :]
            out_ref[k] = (a + b.astype(F32)).astype(BF)

    out = jax.ShapeDtypeStruct((8, BLOCK, 2 * HEAD), BF)
    return local(kernel, out, "join", 0, at, own1, own2, got1, got2)


def input_grads(at, dd, dp, weights, quarters, first, second, types):
    width = weights[0].shape[1] // 4

    def kernel(at, dd_ref, dp_ref, w0, w1, *refs):
        w, (out1_ref, out2_ref) = refs[:8], refs[8:]
        own = jnp.concatenate([dd_ref[first], dd_ref[second]], 0)
        other = jnp.concatenate([dp_ref[(first + 4) % 8], dp_ref[(second + 4) % 8]], 0)
        for r in range(4):
            cols = lanes((at[PLACE_X] + r) % 4, width)
            out = jnp.dot(own, jnp.concatenate([w0[:, cols], w1[:, cols]], 0), preferred_element_type=F32)
            out += jnp.dot(other, jnp.concatenate([w[r][...], w[4 + r][...]], 0), preferred_element_type=F32)
            out1_ref[:, cols] = out[:BLOCK].astype(out1_ref.dtype)
            out2_ref[:, cols] = out[BLOCK:].astype(out2_ref.dtype)

    out = [struct(BLOCK, 4 * width, t) for t in types]
    return local(kernel, out, "input_grads", 0, at, dd, dp, *weights, *quarters)


def spread(at, here, up, down, cross):
    rows, width = here.shape[0], here.shape[1] // 4

    def kernel(at, here_ref, up_ref, down_ref, cross_ref, out_ref):
        h = at[PLACE_H]
        for k in range(4):
            cols = slice(width * k, width * (k + 1))
            total = here_ref[:, cols] + up_ref[:, cols].astype(F32) + down_ref[:, cols].astype(F32)
            out_ref[:, lanes(2 * k + h, width)] = total.astype(BF)
            out_ref[:, lanes(2 * k + 1 - h, width)] = cross_ref[:, cols]

    return local(kernel, struct(rows, 8 * width), "spread", 0, at, here, up, down, cross)


def body(inputs, queries, d_attn, w_key, w_value):
    x, l, z, h, c = (lax.axis_index(name) for name in ("x", "l", "z", "h", "c"))
    at = jnp.stack([x, z, h, c, l]).astype(jnp.int32)

    own, theirs = pick_inputs(at, inputs)
    q = pair(theirs, "h")
    a = ring(own, "z", 1)
    b = ring(own, "z", -1)
    quarter, w_mine = pick_weights(at, after(w_key, own).T, w_value.T)
    wq = pair(quarter, "h")
    w_other = pair(w_mine, "c")
    o0 = ring(a[:32], "z", 1)
    o1 = ring(b[32:], "z", -1)
    q = after(q, o0, o1)
    qa = ring(q, "z", 1)
    qb = ring(q, "z", -1)
    quarters = [wq, ring(wq, "x", -1), ring(wq, "x", 2), ring(wq, "x", 1)]
    quarters += [pair(w, "c") for w in quarters]
    qo0 = ring(qa[:32], "z", 1)
    qo1 = ring(qb[32:], "z", -1)
    group1 = (own, b, a, q)
    group2 = (o0, o1, qb, qo0, qo1, qa)
    send1 = project_partner(at, quarters, group1)
    got1 = pair(send1, "h")
    send2 = project_partner(at, quarters, group2)
    got2 = pair(send2, "h")
    own1 = project_own(at, (w_mine, w_other), (after(own, send2),) + group1[1:])
    own2 = project_own(at, (w_mine, w_other), (after(o0, send2),) + group2[1:])
    kv = join(at, own1, own2, got1, got2)
    (x_own,) = stack(at, ((own, b, o0, o1, after(a, kv), q, qb, qo0, qo1, qa),), "stack_tokens")
    kv_other = pair(kv, "c")
    x_own, kv_other = lax.optimization_barrier((x_own, kv_other))
    x_other = pair(x_own, "c")
    d_query, d_own, d_mine, d_send = attention(at, queries.T, d_attn.T, kv, kv_other)
    dd, dd_other = merge(at, d_own, d_mine, pair(d_send, "c"))
    dp = pair(dd, "h")

    weights = (w_mine, w_other)

    def add(first, second):
        return (first + second.astype(F32)).astype(BF)

    def sum_up(first, *others):
        total = first.astype(F32)
        for other in others:
            total = total + other.astype(F32)
        return total.astype(BF)

    x_other = after(x_other, d_send)
    far_o, dn_o, up_o, own_o = weight_grads(at, dd, dd_other, x_own, x_other, False, (2, 3, 1, 0))
    dp = after(dp, far_o)
    far_o = ring(far_o, "x", 1)
    dn_o = ring(dn_o, "x", -1)
    t2, t1 = input_grads(at, dd, dp, weights, quarters, 6, 7, (BF, BF))
    up2 = ring(t2, "z", 1)
    dn1 = ring(t1, "z", -1)
    dp_other = pair(dp[:, :, HEAD:], "c")
    far_p, up_p, dn_p, own_p = weight_grads(at, dp, after(dp_other, t1), x_own, x_other, True, (2, 1, 3, 0))
    ddb = after(dd, far_p, far_o, dn_o)
    far_p = ring(far_p, "x", -1)
    up_o = ring(sum_up(up_o, far_o), "x", 1)
    u1, t2 = input_grads(at, ddb, dp, weights, quarters, 5, 2, (F32, BF))
    dn2 = ring(t2, "z", -1)
    ddc = after(ddb, up2, dn1)
    up1 = ring(add(u1, up2), "z", 1)
    u0, d0 = input_grads(at, ddc, dp, weights, quarters, 1, 3, (BF, F32))
    cr, here = input_grads(at, ddc, dp, weights, quarters, 4, 0, (F32, F32))
    up_p = ring(after(up_p, up_o), "x", 1)
    dn_p = ring(sum_up(dn_p, far_p), "x", -1)
    up0 = ring(after(u0, up1), "z", 1)
    dn0 = ring(add(d0, dn2), "z", -1)
    total_o = sum_up(own_o, up_o, dn_o)
    fin_o = lax.ppermute(total_o, ("l", "h"), [(2, 0), (1, 3)])
    cross = pair(after(add(cr + up1.astype(F32), dn1), fin_o), "h")
    total_p = after(sum_up(own_p, up_p, dn_p), up1, dn1)
    fin_p = lax.ppermute(total_p, ("l", "h"), [(0, 1), (3, 2)])
    fin_q = lax.ppermute(total_p, ("l", "h"), [(2, 1), (1, 2)])
    d_input = spread(at, here, up0, dn0, cross)
    g_key, g_value = finish(after(at, d_input), total_o, fin_o, fin_p, fin_q)
    return d_input, d_query.T, g_key.T, g_value.T


def solution(mesh):
    fine = Mesh(mesh.devices.reshape(4, 2, 4, 2, 2), ("x", "l", "z", "h", "c"))
    dp, tensor = ("x", "l"), ("z", "h", "c")
    return jax.shard_map(
        body,
        mesh=fine,
        in_specs=(P(dp + tensor, None), P(dp, tensor), P(dp, tensor), P(None, tensor), P(None, tensor)),
        out_specs=(P(dp + tensor, None), P(dp, tensor), P(dp, tensor), P(dp, tensor)),
        check_vma=False,
    )
```

```python
import functools

import jax
import jax.numpy as jnp
from jax import lax
from jax.experimental import pallas as pl
from jax.experimental.pallas import tpu as pltpu
from jax.sharding import Mesh, PartitionSpec as P

HEAD = 192
HALF = 96
BLOCK = 64
ROWS = 256
BF = jnp.bfloat16
F32 = jnp.float32
VM = pl.BlockSpec(memory_space=pltpu.VMEM)
PLACE_X, PLACE_Z, PLACE_H, PLACE_C, PLACE_L = range(5)


def ring(value, axis, step):
    return lax.ppermute(value, axis, [(i, (i + step) % 4) for i in range(4)])


def pair(value, axis):
    return lax.ppermute(value, axis, [(0, 1), (1, 0)])


def after(value, *others):
    return lax.optimization_barrier((value, *others))[0]


def attn_kernel(at, q_ref, g_ref, own_ref, oth_ref, dq_ref, own_out, mine_out, send_out, kt, vt, kn, dkt, dvt):
    core, z, h = at[PLACE_C], at[PLACE_Z], at[PLACE_H]
    step = pl.program_id(0)
    lo = pl.multiple_of(core * HALF, HALF)
    hi = pl.multiple_of(HALF - core * HALF, HALF)
    scale = HEAD ** -0.5

    def place(chip):
        return ((chip // 2 + 4 - z) % 4) + 4 * ((chip % 2 + h) % 2)

    @pl.when(step == 0)
    def _():
        for half, ref, a, b in ((0, own_ref, lo, hi), (1, oth_ref, hi, lo)):
            for jj in range(4):
                blk = jnp.concatenate([ref[place(2 * jj)], ref[place(2 * jj + 1)]], 0)
                t = blk.T
                col = slice(256 * jj + 128 * half, 256 * jj + 128 * half + 128)
                kt[pl.ds(a, HALF), col] = t[0:96]
                vt[pl.ds(a, HALF), col] = t[96:192]
                kt[pl.ds(b, HALF), col] = t[192:288]
                vt[pl.ds(b, HALF), col] = t[288:384]
        kn[...] = kt[...].T
        dkt[...] = jnp.zeros_like(dkt)
        dvt[...] = jnp.zeros_like(dvt)

    row = lax.broadcasted_iota(jnp.int32, (ROWS, 256), 0)
    col = lax.broadcasted_iota(jnp.int32, (ROWS, 256), 1)
    parity = jnp.where(col < 128, core, 1 - core)
    pos = ((col % 128) // 64) * 128 + parity * 64 + col % 64
    mask = row >= pos

    def block(i):
        width = 256 * (i + 1)
        for j in range(3):
            qt = q_ref[HEAD * j:HEAD * (j + 1), :]
            gt = g_ref[HEAD * j:HEAD * (j + 1), :]
            s = jnp.dot(qt.T, kt[:, :width], preferred_element_type=F32)
            last = jnp.where(mask, s[:, width - 256:], -jnp.inf)
            s = last if i == 0 else jnp.concatenate([s[:, :width - 256], last], 1)
            top = jnp.max(s, -1, keepdims=True)
            p = jnp.exp2((s - top) * (scale * 1.4426950408889634))
            inv = 1.0 / jnp.sum(p, -1, keepdims=True)
            dp = jnp.dot(gt.T, vt[:, :width], preferred_element_type=F32)
            total = jnp.sum(p * dp, -1, keepdims=True) * inv
            ds = (p * (dp - total)).astype(BF)
            dq = jnp.dot(ds, kn[:width, :], preferred_element_type=F32) * (inv * scale)
            dq_ref[HEAD * j:HEAD * (j + 1), :] = dq.astype(BF).T
            along = jnp.broadcast_to(inv, (ROWS, 128)).T[0:1, :]
            qs = (qt.astype(F32) * (along * scale)).astype(BF)
            gs = (gt.astype(F32) * along).astype(BF)
            dkt[:, :width] += jnp.dot(qs, ds, preferred_element_type=F32)
            dvt[:, :width] += jnp.dot(gs, p.astype(BF), preferred_element_type=F32)

    for i in range(4):
        pl.when(step == i)(functools.partial(block, i))

    @pl.when(step == 3)
    def _():
        for half, a, b in ((0, lo, hi), (1, hi, lo)):
            for jj in range(4):
                col = slice(256 * jj + 128 * half, 256 * jj + 128 * half + 128)
                t = jnp.concatenate(
                    [dkt[pl.ds(a, HALF), col], dvt[pl.ds(a, HALF), col], dkt[pl.ds(b, HALF), col], dvt[pl.ds(b, HALF), col]], 0
                ).T
                for n in range(2):
                    to, part = place(2 * jj + n), t[64 * n:64 * (n + 1)]
                    if half == 0:
                        own_out[to] = part
                        send_out[to, :, 2 * HEAD:] = part[:, HEAD:].astype(BF)
                    else:
                        send_out[to, :, :2 * HEAD] = part.astype(BF)
                        mine_out[to] = part[:, HEAD:]


def attention(at, queries, d_attn, own, oth):
    rows = pl.BlockSpec((queries.shape[0], ROWS), lambda i, at: (0, i))

    def spec(columns):
        return pl.BlockSpec((8, BLOCK, columns), lambda i, at: (0, 0, 0))

    whole = spec(2 * HEAD)
    return pl.pallas_call(
        attn_kernel,
        grid_spec=pltpu.PrefetchScalarGridSpec(
            num_scalar_prefetch=1,
            grid=(queries.shape[1] // ROWS,),
            in_specs=[rows, rows, whole, whole],
            out_specs=[rows, whole, spec(HEAD), spec(3 * HEAD)],
            scratch_shapes=[
                pltpu.VMEM((HEAD, 1024), BF),
                pltpu.VMEM((HEAD, 1024), BF),
                pltpu.VMEM((1024, HEAD), BF),
                pltpu.VMEM((HEAD, 1024), F32),
                pltpu.VMEM((HEAD, 1024), F32),
            ],
        ),
        out_shape=[
            jax.ShapeDtypeStruct(queries.shape, BF),
            jax.ShapeDtypeStruct((8, BLOCK, 2 * HEAD), F32),
            jax.ShapeDtypeStruct((8, BLOCK, HEAD), F32),
            jax.ShapeDtypeStruct((8, BLOCK, 3 * HEAD), BF),
        ],
        compiler_params=pltpu.CompilerParams(vmem_limit_bytes=28 * 1024 * 1024),
        cost_estimate=pl.CostEstimate(flops=8 * 10**9, bytes_accessed=6 * 10**6, transcendentals=2 * 10**6),
        name="attention",
    )(at, queries, d_attn, own, oth)


def local(kernel, out_shape, name, semaphores, *args):
    many = isinstance(out_shape, list)
    ins = pl.BlockSpec(memory_space=pl.ANY) if semaphores else VM
    return pl.pallas_call(
        kernel,
        in_specs=[pl.BlockSpec(memory_space=pltpu.SMEM)] + [ins] * (len(args) - 1),
        out_specs=[VM] * len(out_shape) if many else VM,
        out_shape=out_shape,
        scratch_shapes=[pltpu.SemaphoreType.DMA((semaphores,))] if semaphores else [],
        compiler_params=pltpu.CompilerParams(vmem_limit_bytes=24 * 1024 * 1024),
        cost_estimate=pl.CostEstimate(flops=1000, bytes_accessed=1000, transcendentals=0),
        name=name,
    )(*args)


def struct(rows, columns, dtype=BF):
    return jax.ShapeDtypeStruct((rows, columns), dtype)


def lanes(index, width):
    return pl.ds(pl.multiple_of(index * width, width), width)


def copies(pairs, sem):
    started = [pltpu.make_async_copy(a, b, sem.at[n]) for n, (a, b) in enumerate(pairs)]
    for copy in started:
        copy.start()
    for copy in started:
        copy.wait()


def pick_inputs(at, inputs):
    rows, width = inputs.shape[0], inputs.shape[1] // 8

    def kernel(at, in_ref, own_ref, theirs_ref):
        h = at[PLACE_H]
        for k in range(4):
            cols = slice(width * k, width * (k + 1))
            theirs_ref[:, cols] = in_ref[:, lanes(2 * k + 1 - h, width)]
            own_ref[:, cols] = in_ref[:, lanes(2 * k + h, width)]

    return local(kernel, [struct(rows, 4 * width)] * 2, "pick_inputs", 0, at, inputs)


def pick_weights(at, w_key, w_value):
    width = w_key.shape[1] // 8

    def kernel(at, key_ref, value_ref, quarter_ref, mine_ref):
        h, x = at[PLACE_H], at[PLACE_X]
        for n, ref in enumerate((key_ref, value_ref)):
            rows = slice(HALF * n, HALF * (n + 1))
            quarter_ref[rows, :] = ref[:, lanes(2 * x + 1 - h, width)]
            for k in range(4):
                mine_ref[rows, width * k:width * (k + 1)] = ref[:, lanes(2 * k + h, width)]

    out = [struct(HEAD, width), struct(HEAD, 4 * width)]
    return local(kernel, out, "pick_weights", 0, at, w_key, w_value)


def project_own(at, weights, pieces):
    rows = sum(p.shape[0] for p in pieces)
    width = pieces[0].shape[1] // 4

    def kernel(at, mine, other, *refs):
        xs, out_ref = refs[:-1], refs[-1]
        for k in range(4):
            cols = slice(width * k, width * (k + 1))
            x = jnp.concatenate([r[:, cols] for r in xs], 0)
            w = jnp.concatenate([mine[:, cols], other[:, cols]], 0)
            part = lax.dot_general(w, x, (((1,), (1,)), ((), ())), preferred_element_type=F32)
            total = part if k == 0 else total + part
        out_ref[...] = total.T

    return local(kernel, struct(rows, 2 * HEAD, F32), "project_own", 0, at, *weights, *pieces)


def project_partner(at, quarters, pieces):
    rows = sum(p.shape[0] for p in pieces)
    width = pieces[0].shape[1] // 4

    def kernel(at, *refs):
        w, xs, out_ref = refs[:8], refs[8:-1], refs[-1]
        for r in range(4):
            cols = lanes((at[PLACE_X] + r) % 4, width)
            x = jnp.concatenate([ref[:, cols] for ref in xs], 0)
            both = jnp.concatenate([w[r][...], w[4 + r][...]], 0)
            part = lax.dot_general(both, x, (((1,), (1,)), ((), ())), preferred_element_type=F32)
            total = part if r == 0 else total + part
        out_ref[...] = total.T.astype(BF)

    return local(kernel, struct(rows, 2 * HEAD), "project_partner", 0, at, *quarters, *pieces)


def merge(at, own, mine, got):
    def kernel(at, own_ref, mine_ref, got_ref, dd_ref, other_ref):
        for k in range(8):
            dd_ref[k] = (own_ref[k] + got_ref[k, :, :2 * HEAD].astype(F32)).astype(BF)
            other_ref[k] = (mine_ref[k] + got_ref[k, :, 2 * HEAD:].astype(F32)).astype(BF)

    out = [jax.ShapeDtypeStruct((8, BLOCK, n * HEAD), BF) for n in (2, 1)]
    return local(kernel, out, "merge", 0, at, own, mine, got)


def stack(at, groups, name):
    rows = [sum(p.shape[0] for p in g) for g in groups]
    width = groups[0][0].shape[1]
    count = [len(g) for g in groups]

    def kernel(at, *refs):
        ins, outs = refs[:sum(count)], refs[sum(count):]
        n = 0
        for out, many in zip(outs, count):
            row = 0
            for ref in ins[n:n + many]:
                out[row:row + ref.shape[0], :] = ref[...]
                row += ref.shape[0]
            n += many

    return local(kernel, [struct(r, width) for r in rows], name, 0, at, *[p for g in groups for p in g])


def weight_grads(at, dd, other, own_x, other_x, swapped, order):
    width = own_x.shape[1] // 4

    def kernel(at, dd_ref, other_ref, x_ref, ox_ref, *outs):
        def turned(ref):
            return jnp.concatenate([ref[(k + 4 * swapped) % 8][:, :HEAD] for k in range(8)], 0).T

        a, b = turned(dd_ref), turned(other_ref)
        for n, r in enumerate(order):
            cols = lanes((at[PLACE_X] + r) % 4, width)
            out = jnp.dot(a, x_ref[:, cols], preferred_element_type=F32)
            out += jnp.dot(b, ox_ref[:, cols], preferred_element_type=F32)
            outs[n][...] = out.astype(BF)

    return local(kernel, [struct(HEAD, width)] * 4, "weight_grads", 0, at, dd, other, own_x, other_x)


def finish(at, own, got_own, got_p, got_q):
    def kernel(at, own_ref, a_ref, b_ref, c_ref, key_ref, value_ref):
        same = at[PLACE_H] == at[PLACE_L]
        mine = own_ref[...].astype(F32) + a_ref[...].astype(F32)
        total = jnp.where(same, mine, b_ref[...].astype(F32) + c_ref[...].astype(F32))
        key_ref[...] = total[:HALF]
        value_ref[...] = total[HALF:]

    return local(kernel, [struct(HALF, own.shape[1], F32)] * 2, "finish", 0, at, own, got_own, got_p, got_q)


def join(at, own1, own2, got1, got2):
    mine = ((0, 0), (0, 1), (1, 0), (0, 2), (0, 3), (1, 1), (1, 2), (1, 3))
    theirs = ((0, 3), (1, 1), (1, 2), (1, 3), (0, 0), (0, 1), (1, 0), (0, 2))

    def kernel(at, own1_ref, own2_ref, got1_ref, got2_ref, out_ref):
        own, got = (own1_ref, own2_ref), (got1_ref, got2_ref)
        for k in range(8):
            (n, i), (m, j) = mine[k], theirs[k]
            a = own[n][BLOCK * i:BLOCK * (i + 1), :]
            b = got[m][BLOCK * j:BLOCK * (j + 1), :]
            out_ref[k] = (a + b.astype(F32)).astype(BF)

    out = jax.ShapeDtypeStruct((8, BLOCK, 2 * HEAD), BF)
    return local(kernel, out, "join", 0, at, own1, own2, got1, got2)


def input_grads(at, dd, dp, weights, quarters, first, second, types):
    width = weights[0].shape[1] // 4

    def kernel(at, dd_ref, dp_ref, w0, w1, *refs):
        w, (out1_ref, out2_ref) = refs[:8], refs[8:]
        own = jnp.concatenate([dd_ref[first], dd_ref[second]], 0)
        other = jnp.concatenate([dp_ref[(first + 4) % 8], dp_ref[(second + 4) % 8]], 0)
        for r in range(4):
            cols = lanes((at[PLACE_X] + r) % 4, width)
            out = jnp.dot(own, jnp.concatenate([w0[:, cols], w1[:, cols]], 0), preferred_element_type=F32)
            out += jnp.dot(other, jnp.concatenate([w[r][...], w[4 + r][...]], 0), preferred_element_type=F32)
            out1_ref[:, cols] = out[:BLOCK].astype(out1_ref.dtype)
            out2_ref[:, cols] = out[BLOCK:].astype(out2_ref.dtype)

    out = [struct(BLOCK, 4 * width, t) for t in types]
    return local(kernel, out, "input_grads", 0, at, dd, dp, *weights, *quarters)


def add_far(at, first, second, up, down):
    half = up.shape[0]

    def kernel(at, first_ref, second_ref, up_ref, down_ref, out1_ref, out2_ref):
        a, b = first_ref[...], second_ref[...]
        out1_ref[:half, :] = (a[:half] + up_ref[...].astype(F32)).astype(BF)
        out1_ref[half:, :] = a[half:].astype(BF)
        out2_ref[:half, :] = b[:half].astype(BF)
        out2_ref[half:, :] = (b[half:] + down_ref[...].astype(F32)).astype(BF)

    return local(kernel, [struct(*first.shape)] * 2, "add_far", 0, at, first, second, up, down)


def spread(at, here, up, down, cross):
    rows, width = here.shape[0], here.shape[1] // 4

    def kernel(at, here_ref, up_ref, down_ref, cross_ref, out_ref):
        h = at[PLACE_H]
        for k in range(4):
            cols = slice(width * k, width * (k + 1))
            total = here_ref[:, cols] + up_ref[:, cols].astype(F32) + down_ref[:, cols].astype(F32)
            out_ref[:, lanes(2 * k + h, width)] = total.astype(BF)
            out_ref[:, lanes(2 * k + 1 - h, width)] = cross_ref[:, cols]

    return local(kernel, struct(rows, 8 * width), "spread", 0, at, here, up, down, cross)


def body(inputs, queries, d_attn, w_key, w_value):
    x, l, z, h, c = (lax.axis_index(name) for name in ("x", "l", "z", "h", "c"))
    at = jnp.stack([x, z, h, c, l]).astype(jnp.int32)

    own, theirs = pick_inputs(at, inputs)
    q = pair(theirs, "h")
    a = ring(own, "z", 1)
    b = ring(own, "z", -1)
    quarter, w_mine = pick_weights(at, after(w_key, own).T, w_value.T)
    wq = pair(quarter, "h")
    w_other = pair(w_mine, "c")
    o0 = ring(a[:32], "z", 1)
    o1 = ring(b[32:], "z", -1)
    q = after(q, o0, o1)
    qa = ring(q, "z", 1)
    qb = ring(q, "z", -1)
    quarters = [wq, ring(wq, "x", -1), ring(wq, "x", 2), ring(wq, "x", 1)]
    quarters += [pair(w, "c") for w in quarters]
    qo0 = ring(qa[:32], "z", 1)
    qo1 = ring(qb[32:], "z", -1)
    group1 = (own, b, a, q)
    group2 = (o0, o1, qb, qo0, qo1, qa)
    send1 = project_partner(at, quarters, group1)
    got1 = pair(send1, "h")
    send2 = project_partner(at, quarters, group2)
    got2 = pair(send2, "h")
    own1 = project_own(at, (w_mine, w_other), (after(own, send2),) + group1[1:])
    own2 = project_own(at, (w_mine, w_other), (after(o0, send2),) + group2[1:])
    kv = join(at, own1, own2, got1, got2)
    (x_own,) = stack(at, ((own, b, o0, o1, after(a, kv), q, qb, qo0, qo1, qa),), "stack_tokens")
    kv_other = pair(kv, "c")
    x_own, kv_other = lax.optimization_barrier((x_own, kv_other))
    x_other = pair(x_own, "c")
    d_query, d_own, d_mine, d_send = attention(at, queries.T, d_attn.T, kv, kv_other)
    dd, dd_other = merge(at, d_own, d_mine, pair(d_send, "c"))
    dp = pair(dd, "h")

    weights = (w_mine, w_other)

    def add(first, second):
        return (first + second.astype(F32)).astype(BF)

    def sum_up(first, *others):
        total = first.astype(F32)
        for other in others:
            total = total + other.astype(F32)
        return total.astype(BF)

    x_other = after(x_other, d_send)
    far_o, dn_o, up_o, own_o = weight_grads(at, dd, dd_other, x_own, x_other, False, (2, 3, 1, 0))
    dp = after(dp, far_o)
    far_o = ring(far_o, "x", 1)
    dn_o = ring(dn_o, "x", -1)
    p2, o2 = input_grads(at, dd, dp, weights, quarters, 6, 2, (BF, BF))
    p2u = ring(p2[:32], "z", 1)
    p2d = ring(p2[32:], "z", -1)
    dp_other = pair(dp[:, :, HEAD:], "c")
    far_p, up_p, dn_p, own_p = weight_grads(at, dp, after(dp_other, p2), x_own, x_other, True, (2, 1, 3, 0))
    ddb = after(dd, far_p)
    far_p = ring(far_p, "x", -1)
    up_o = ring(sum_up(up_o, far_o), "x", 1)
    p1, p3 = input_grads(at, ddb, dp, weights, quarters, 5, 7, (F32, F32))
    p1, p3 = add_far(at, p1, p3, p2u, p2d)
    p1 = ring(p1, "z", 1)
    p3 = ring(p3, "z", -1)
    ddc = after(ddb, far_o)
    o1, o3 = input_grads(at, ddc, dp, weights, quarters, 1, 3, (F32, F32))
    cr, here = input_grads(at, ddc, dp, weights, quarters, 4, 0, (F32, F32))
    dn_p = ring(sum_up(dn_p, far_p), "x", -1)
    total_o = sum_up(own_o, up_o, dn_o)
    fin_o = lax.ppermute(total_o, ("l", "h"), [(2, 0), (1, 3)])
    up_p = ring(after(up_p, up_o), "x", 1)
    o2 = after(o2, p1, p3)
    o2u = ring(o2[:32], "z", 1)
    o2d = ring(o2[32:], "z", -1)
    cross = pair(add(cr + p1.astype(F32), p3), "h")
    o1, o3 = add_far(at, o1, o3, o2u, o2d)
    up0 = ring(o1, "z", 1)
    dn0 = ring(o3, "z", -1)
    total_p = after(sum_up(own_p, up_p, dn_p), o2u, o2d)
    fin_p = lax.ppermute(total_p, ("l", "h"), [(0, 1), (3, 2)])
    fin_q = lax.ppermute(total_p, ("l", "h"), [(2, 1), (1, 2)])
    d_input = spread(at, here, up0, dn0, cross)
    g_key, g_value = finish(after(at, d_input), total_o, fin_o, fin_p, fin_q)
    return d_input, d_query.T, g_key.T, g_value.T


def solution(mesh):
    fine = Mesh(mesh.devices.reshape(4, 2, 4, 2, 2), ("x", "l", "z", "h", "c"))
    dp, tensor = ("x", "l"), ("z", "h", "c")
    return jax.shard_map(
        body,
        mesh=fine,
        in_specs=(P(dp + tensor, None), P(dp, tensor), P(dp, tensor), P(None, tensor), P(None, tensor)),
        out_specs=(P(dp + tensor, None), P(dp, tensor), P(dp, tensor), P(dp, tensor)),
        check_vma=False,
    )
```

```python
import functools

import jax
import jax.numpy as jnp
from jax import lax
from jax.experimental import pallas as pl
from jax.experimental.pallas import tpu as pltpu
from jax.sharding import Mesh, PartitionSpec as P

HEAD = 192
HALF = 96
BLOCK = 64
ROWS = 256
BF = jnp.bfloat16
F32 = jnp.float32
VM = pl.BlockSpec(memory_space=pltpu.VMEM)
PLACE_X, PLACE_Z, PLACE_H, PLACE_C, PLACE_L = range(5)


def ring(value, axis, step):
    return lax.ppermute(value, axis, [(i, (i + step) % 4) for i in range(4)])


def pair(value, axis):
    return lax.ppermute(value, axis, [(0, 1), (1, 0)])


def after(value, *others):
    return lax.optimization_barrier((value, *others))[0]


def attn_kernel(at, q_ref, g_ref, own_ref, oth_ref, dq_ref, own_out, mine_out, send_out, kt, vt, kn, dkt, dvt):
    core, z, h = at[PLACE_C], at[PLACE_Z], at[PLACE_H]
    step = pl.program_id(0)
    lo = pl.multiple_of(core * HALF, HALF)
    hi = pl.multiple_of(HALF - core * HALF, HALF)
    scale = HEAD ** -0.5

    def place(chip):
        return ((chip // 2 + 4 - z) % 4) + 4 * ((chip % 2 + h) % 2)

    @pl.when(step == 0)
    def _():
        for half, ref, a, b in ((0, own_ref, lo, hi), (1, oth_ref, hi, lo)):
            for jj in range(4):
                blk = jnp.concatenate([ref[place(2 * jj)], ref[place(2 * jj + 1)]], 0)
                t = blk.T
                col = slice(256 * jj + 128 * half, 256 * jj + 128 * half + 128)
                kt[pl.ds(a, HALF), col] = t[0:96]
                vt[pl.ds(a, HALF), col] = t[96:192]
                kt[pl.ds(b, HALF), col] = t[192:288]
                vt[pl.ds(b, HALF), col] = t[288:384]
        kn[...] = kt[...].T
        dkt[...] = jnp.zeros_like(dkt)
        dvt[...] = jnp.zeros_like(dvt)

    row = lax.broadcasted_iota(jnp.int32, (ROWS, 256), 0)
    col = lax.broadcasted_iota(jnp.int32, (ROWS, 256), 1)
    parity = jnp.where(col < 128, core, 1 - core)
    pos = ((col % 128) // 64) * 128 + parity * 64 + col % 64
    mask = row >= pos

    def block(i):
        width = 256 * (i + 1)
        for j in range(3):
            qt = q_ref[HEAD * j:HEAD * (j + 1), :]
            gt = g_ref[HEAD * j:HEAD * (j + 1), :]
            s = jnp.dot(qt.T, kt[:, :width], preferred_element_type=F32)
            last = jnp.where(mask, s[:, width - 256:], -jnp.inf)
            s = last if i == 0 else jnp.concatenate([s[:, :width - 256], last], 1)
            top = jnp.max(s, -1, keepdims=True)
            p = jnp.exp2((s - top) * (scale * 1.4426950408889634))
            inv = 1.0 / jnp.sum(p, -1, keepdims=True)
            dp = jnp.dot(gt.T, vt[:, :width], preferred_element_type=F32)
            total = jnp.sum(p * dp, -1, keepdims=True) * inv
            ds = (p * (dp - total)).astype(BF)
            dq = jnp.dot(ds, kn[:width, :], preferred_element_type=F32) * (inv * scale)
            dq_ref[HEAD * j:HEAD * (j + 1), :] = dq.astype(BF).T
            along = jnp.broadcast_to(inv, (ROWS, 128)).T[0:1, :]
            qs = (qt.astype(F32) * (along * scale)).astype(BF)
            gs = (gt.astype(F32) * along).astype(BF)
            dkt[:, :width] += jnp.dot(qs, ds, preferred_element_type=F32)
            dvt[:, :width] += jnp.dot(gs, p.astype(BF), preferred_element_type=F32)

    for i in range(4):
        pl.when(step == i)(functools.partial(block, i))

    @pl.when(step == 3)
    def _():
        for half, a, b in ((0, lo, hi), (1, hi, lo)):
            for jj in range(4):
                col = slice(256 * jj + 128 * half, 256 * jj + 128 * half + 128)
                t = jnp.concatenate(
                    [dkt[pl.ds(a, HALF), col], dvt[pl.ds(a, HALF), col], dkt[pl.ds(b, HALF), col], dvt[pl.ds(b, HALF), col]], 0
                ).T
                for n in range(2):
                    to, part = place(2 * jj + n), t[64 * n:64 * (n + 1)]
                    if half == 0:
                        own_out[to] = part
                        send_out[to, :, 2 * HEAD:] = part[:, HEAD:].astype(BF)
                    else:
                        send_out[to, :, :2 * HEAD] = part.astype(BF)
                        mine_out[to] = part[:, HEAD:]


def attention(at, queries, d_attn, own, oth):
    rows = pl.BlockSpec((queries.shape[0], ROWS), lambda i, at: (0, i))

    def spec(columns):
        return pl.BlockSpec((8, BLOCK, columns), lambda i, at: (0, 0, 0))

    whole = spec(2 * HEAD)
    return pl.pallas_call(
        attn_kernel,
        grid_spec=pltpu.PrefetchScalarGridSpec(
            num_scalar_prefetch=1,
            grid=(queries.shape[1] // ROWS,),
            in_specs=[rows, rows, whole, whole],
            out_specs=[rows, whole, spec(HEAD), spec(3 * HEAD)],
            scratch_shapes=[
                pltpu.VMEM((HEAD, 1024), BF),
                pltpu.VMEM((HEAD, 1024), BF),
                pltpu.VMEM((1024, HEAD), BF),
                pltpu.VMEM((HEAD, 1024), F32),
                pltpu.VMEM((HEAD, 1024), F32),
            ],
        ),
        out_shape=[
            jax.ShapeDtypeStruct(queries.shape, BF),
            jax.ShapeDtypeStruct((8, BLOCK, 2 * HEAD), F32),
            jax.ShapeDtypeStruct((8, BLOCK, HEAD), F32),
            jax.ShapeDtypeStruct((8, BLOCK, 3 * HEAD), BF),
        ],
        compiler_params=pltpu.CompilerParams(vmem_limit_bytes=28 * 1024 * 1024),
        cost_estimate=pl.CostEstimate(flops=8 * 10**9, bytes_accessed=6 * 10**6, transcendentals=2 * 10**6),
        name="attention",
    )(at, queries, d_attn, own, oth)


def local(kernel, out_shape, name, semaphores, *args):
    many = isinstance(out_shape, list)
    ins = pl.BlockSpec(memory_space=pl.ANY) if semaphores else VM
    return pl.pallas_call(
        kernel,
        in_specs=[pl.BlockSpec(memory_space=pltpu.SMEM)] + [ins] * (len(args) - 1),
        out_specs=[VM] * len(out_shape) if many else VM,
        out_shape=out_shape,
        scratch_shapes=[pltpu.SemaphoreType.DMA((semaphores,))] if semaphores else [],
        compiler_params=pltpu.CompilerParams(vmem_limit_bytes=24 * 1024 * 1024),
        cost_estimate=pl.CostEstimate(flops=1000, bytes_accessed=1000, transcendentals=0),
        name=name,
    )(*args)


def struct(rows, columns, dtype=BF):
    return jax.ShapeDtypeStruct((rows, columns), dtype)


def lanes(index, width):
    return pl.ds(pl.multiple_of(index * width, width), width)


def copies(pairs, sem):
    started = [pltpu.make_async_copy(a, b, sem.at[n]) for n, (a, b) in enumerate(pairs)]
    for copy in started:
        copy.start()
    for copy in started:
        copy.wait()


def pick_inputs(at, inputs):
    rows, width = inputs.shape[0], inputs.shape[1] // 8

    def kernel(at, in_ref, own_ref, theirs_ref):
        h = at[PLACE_H]
        for k in range(4):
            cols = slice(width * k, width * (k + 1))
            theirs_ref[:, cols] = in_ref[:, lanes(2 * k + 1 - h, width)]
            own_ref[:, cols] = in_ref[:, lanes(2 * k + h, width)]

    return local(kernel, [struct(rows, 4 * width)] * 2, "pick_inputs", 0, at, inputs)


def pick_weights(at, w_key, w_value):
    width = w_key.shape[1] // 8

    def kernel(at, key_ref, value_ref, quarter_ref, mine_ref):
        h, x = at[PLACE_H], at[PLACE_X]
        for n, ref in enumerate((key_ref, value_ref)):
            rows = slice(HALF * n, HALF * (n + 1))
            quarter_ref[rows, :] = ref[:, lanes(2 * x + 1 - h, width)]
            for k in range(4):
                mine_ref[rows, width * k:width * (k + 1)] = ref[:, lanes(2 * k + h, width)]

    out = [struct(HEAD, width), struct(HEAD, 4 * width)]
    return local(kernel, out, "pick_weights", 0, at, w_key, w_value)


def project_own(at, weights, pieces):
    rows = sum(p.shape[0] for p in pieces)
    width = pieces[0].shape[1] // 4

    def kernel(at, mine, other, *refs):
        xs, out_ref = refs[:-1], refs[-1]
        for k in range(4):
            cols = slice(width * k, width * (k + 1))
            x = jnp.concatenate([r[:, cols] for r in xs], 0)
            w = jnp.concatenate([mine[:, cols], other[:, cols]], 0)
            part = lax.dot_general(w, x, (((1,), (1,)), ((), ())), preferred_element_type=F32)
            total = part if k == 0 else total + part
        out_ref[...] = total.T

    return local(kernel, struct(rows, 2 * HEAD, F32), "project_own", 0, at, *weights, *pieces)


def project_partner(at, quarters, pieces):
    rows = sum(p.shape[0] for p in pieces)
    width = pieces[0].shape[1] // 4

    def kernel(at, *refs):
        w, xs, out_ref = refs[:8], refs[8:-1], refs[-1]
        for r in range(4):
            cols = lanes((at[PLACE_X] + r) % 4, width)
            x = jnp.concatenate([ref[:, cols] for ref in xs], 0)
            both = jnp.concatenate([w[r][...], w[4 + r][...]], 0)
            part = lax.dot_general(both, x, (((1,), (1,)), ((), ())), preferred_element_type=F32)
            total = part if r == 0 else total + part
        out_ref[...] = total.T.astype(BF)

    return local(kernel, struct(rows, 2 * HEAD), "project_partner", 0, at, *quarters, *pieces)


def merge(at, own, mine, got):
    def kernel(at, own_ref, mine_ref, got_ref, dd_ref, other_ref):
        for k in range(8):
            dd_ref[k] = (own_ref[k] + got_ref[k, :, :2 * HEAD].astype(F32)).astype(BF)
            other_ref[k] = (mine_ref[k] + got_ref[k, :, 2 * HEAD:].astype(F32)).astype(BF)

    out = [jax.ShapeDtypeStruct((8, BLOCK, n * HEAD), BF) for n in (2, 1)]
    return local(kernel, out, "merge", 0, at, own, mine, got)


def stack(at, groups, name):
    rows = [sum(p.shape[0] for p in g) for g in groups]
    width = groups[0][0].shape[1]
    count = [len(g) for g in groups]

    def kernel(at, *refs):
        ins, outs = refs[:sum(count)], refs[sum(count):]
        n = 0
        for out, many in zip(outs, count):
            row = 0
            for ref in ins[n:n + many]:
                out[row:row + ref.shape[0], :] = ref[...]
                row += ref.shape[0]
            n += many

    return local(kernel, [struct(r, width) for r in rows], name, 0, at, *[p for g in groups for p in g])


def weight_grads(at, dd, other, own_x, other_x, swapped, order):
    width = own_x.shape[1] // 4

    def kernel(at, dd_ref, other_ref, x_ref, ox_ref, *outs):
        def turned(ref):
            return jnp.concatenate([ref[(k + 4 * swapped) % 8][:, :HEAD] for k in range(8)], 0).T

        a, b = turned(dd_ref), turned(other_ref)
        for n, r in enumerate(order):
            cols = lanes((at[PLACE_X] + r) % 4, width)
            out = jnp.dot(a, x_ref[:, cols], preferred_element_type=F32)
            out += jnp.dot(b, ox_ref[:, cols], preferred_element_type=F32)
            outs[n][...] = out.astype(BF)

    return local(kernel, [struct(HEAD, width)] * 4, "weight_grads", 0, at, dd, other, own_x, other_x)


def finish(at, own, got_own, got_p, got_q):
    def kernel(at, own_ref, a_ref, b_ref, c_ref, key_ref, value_ref):
        same = at[PLACE_H] == at[PLACE_L]
        mine = own_ref[...].astype(F32) + a_ref[...].astype(F32)
        total = jnp.where(same, mine, b_ref[...].astype(F32) + c_ref[...].astype(F32))
        key_ref[...] = total[:HALF]
        value_ref[...] = total[HALF:]

    return local(kernel, [struct(HALF, own.shape[1], F32)] * 2, "finish", 0, at, own, got_own, got_p, got_q)


def join(at, own1, own2, got1, got2):
    mine = ((0, 0), (0, 1), (1, 0), (0, 2), (0, 3), (1, 1), (1, 2), (1, 3))
    theirs = ((0, 3), (1, 1), (1, 2), (1, 3), (0, 0), (0, 1), (1, 0), (0, 2))

    def kernel(at, own1_ref, own2_ref, got1_ref, got2_ref, out_ref):
        own, got = (own1_ref, own2_ref), (got1_ref, got2_ref)
        for k in range(8):
            (n, i), (m, j) = mine[k], theirs[k]
            a = own[n][BLOCK * i:BLOCK * (i + 1), :]
            b = got[m][BLOCK * j:BLOCK * (j + 1), :]
            out_ref[k] = (a + b.astype(F32)).astype(BF)

    out = jax.ShapeDtypeStruct((8, BLOCK, 2 * HEAD), BF)
    return local(kernel, out, "join", 0, at, own1, own2, got1, got2)


def input_grads(at, dd, dp, weights, quarters, first, second, types):
    width = weights[0].shape[1] // 4

    def kernel(at, dd_ref, dp_ref, w0, w1, *refs):
        w, (out1_ref, out2_ref) = refs[:8], refs[8:]
        own = jnp.concatenate([dd_ref[first], dd_ref[second]], 0)
        other = jnp.concatenate([dp_ref[(first + 4) % 8], dp_ref[(second + 4) % 8]], 0)
        for r in range(4):
            cols = lanes((at[PLACE_X] + r) % 4, width)
            out = jnp.dot(own, jnp.concatenate([w0[:, cols], w1[:, cols]], 0), preferred_element_type=F32)
            out += jnp.dot(other, jnp.concatenate([w[r][...], w[4 + r][...]], 0), preferred_element_type=F32)
            out1_ref[:, cols] = out[:BLOCK].astype(out1_ref.dtype)
            out2_ref[:, cols] = out[BLOCK:].astype(out2_ref.dtype)

    out = [struct(BLOCK, 4 * width, t) for t in types]
    return local(kernel, out, "input_grads", 0, at, dd, dp, *weights, *quarters)


def add_far(at, first, second, up, down):
    half = up.shape[0]

    def kernel(at, first_ref, second_ref, up_ref, down_ref, out1_ref, out2_ref):
        a, b = first_ref[...], second_ref[...]
        out1_ref[:half, :] = (a[:half] + up_ref[...].astype(F32)).astype(BF)
        out1_ref[half:, :] = a[half:].astype(BF)
        out2_ref[:half, :] = b[:half].astype(BF)
        out2_ref[half:, :] = (b[half:] + down_ref[...].astype(F32)).astype(BF)

    return local(kernel, [struct(*first.shape)] * 2, "add_far", 0, at, first, second, up, down)


def spread(at, here, up, down, cross):
    rows, width = here.shape[0], here.shape[1] // 4

    def kernel(at, here_ref, up_ref, down_ref, cross_ref, out_ref):
        h = at[PLACE_H]
        for k in range(4):
            cols = slice(width * k, width * (k + 1))
            total = here_ref[:, cols] + up_ref[:, cols].astype(F32) + down_ref[:, cols].astype(F32)
            out_ref[:, lanes(2 * k + h, width)] = total.astype(BF)
            out_ref[:, lanes(2 * k + 1 - h, width)] = cross_ref[:, cols]

    return local(kernel, struct(rows, 8 * width), "spread", 0, at, here, up, down, cross)


def body(inputs, queries, d_attn, w_key, w_value):
    x, l, z, h, c = (lax.axis_index(name) for name in ("x", "l", "z", "h", "c"))
    at = jnp.stack([x, z, h, c, l]).astype(jnp.int32)

    own, theirs = pick_inputs(at, inputs)
    q = pair(theirs, "h")
    a = ring(own, "z", 1)
    b = ring(own, "z", -1)
    quarter, w_mine = pick_weights(at, after(w_key, own).T, w_value.T)
    wq = pair(quarter, "h")
    o0 = ring(a[:32], "z", 1)
    o1 = ring(b[32:], "z", -1)
    q = after(q, o0, o1)
    w_other = pair(after(w_mine, wq, q), "c")
    q = after(q, w_other)
    qa = ring(q, "z", 1)
    qb = ring(q, "z", -1)
    quarters = [wq, ring(wq, "x", -1), ring(wq, "x", 2), ring(wq, "x", 1)]
    quarters += [pair(w, "c") for w in quarters]
    qo0 = ring(qa[:32], "z", 1)
    qo1 = ring(qb[32:], "z", -1)
    group1 = (own, b, a, q)
    group2 = (o0, o1, qb, qo0, qo1, qa)
    send1 = project_partner(at, quarters, group1)
    got1 = pair(send1, "h")
    send2 = project_partner(at, quarters, group2)
    got2 = pair(send2, "h")
    own1 = project_own(at, (w_mine, w_other), (after(own, send2),) + group1[1:])
    own2 = project_own(at, (w_mine, w_other), (after(o0, send2),) + group2[1:])
    kv = join(at, own1, own2, got1, got2)
    (x_own,) = stack(at, ((own, b, o0, o1, after(a, kv), q, qb, qo0, qo1, qa),), "stack_tokens")
    kv_other = pair(kv, "c")
    x_own, kv_other = lax.optimization_barrier((x_own, kv_other))
    x_other = pair(x_own, "c")
    d_query, d_own, d_mine, d_send = attention(at, queries.T, d_attn.T, kv, kv_other)
    dd, dd_other = merge(at, d_own, d_mine, pair(d_send, "c"))
    dp = pair(dd, "h")

    weights = (w_mine, w_other)

    def add(first, second):
        return (first + second.astype(F32)).astype(BF)

    def sum_up(first, *others):
        total = first.astype(F32)
        for other in others:
            total = total + other.astype(F32)
        return total.astype(BF)

    x_other = after(x_other, d_send)
    far_o, dn_o, up_o, own_o = weight_grads(at, dd, dd_other, x_own, x_other, False, (2, 3, 1, 0))
    dp = after(dp, far_o)
    far_o = ring(far_o, "x", 1)
    dn_o = ring(dn_o, "x", -1)
    p2, o2 = input_grads(at, dd, dp, weights, quarters, 6, 2, (BF, BF))
    p2u = ring(p2[:32], "z", 1)
    p2d = ring(p2[32:], "z", -1)
    dp_other = pair(dp[:, :, HEAD:], "c")
    far_p, up_p, dn_p, own_p = weight_grads(at, dp, after(dp_other, p2), x_own, x_other, True, (2, 1, 3, 0))
    ddb = after(dd, far_p)
    far_p = ring(far_p, "x", -1)
    up_p = ring(up_p, "x", 1)
    up_o = ring(after(sum_up(up_o, far_o), up_p), "x", 1)
    p1, p3 = input_grads(at, ddb, dp, weights, quarters, 5, 7, (F32, F32))
    p1, p3 = add_far(at, p1, p3, after(p2u, dn_o), p2d)
    p1 = ring(p1, "z", 1)
    p3 = ring(p3, "z", -1)
    ddc = after(ddb, far_o)
    o1, o3 = input_grads(at, ddc, dp, weights, quarters, 1, 3, (F32, F32))
    cr, here = input_grads(at, ddc, dp, weights, quarters, 4, 0, (F32, F32))
    dn_p = ring(sum_up(dn_p, far_p), "x", -1)
    total_o = sum_up(own_o, up_o, dn_o)
    fin_o = lax.ppermute(total_o, ("l", "h"), [(2, 0), (1, 3)])
    o2 = after(o2, p1, p3)
    o2u = ring(o2[:32], "z", 1)
    o2d = ring(o2[32:], "z", -1)
    cross = pair(add(cr + p1.astype(F32), p3), "h")
    o1, o3 = add_far(at, o1, o3, o2u, o2d)
    up0 = ring(o1, "z", 1)
    dn0 = ring(o3, "z", -1)
    total_p = after(sum_up(own_p, up_p, dn_p), o2u, o2d)
    fin_p = lax.ppermute(total_p, ("l", "h"), [(0, 1), (3, 2)])
    fin_q = lax.ppermute(total_p, ("l", "h"), [(2, 1), (1, 2)])
    d_input = spread(at, here, up0, dn0, cross)
    g_key, g_value = finish(after(at, d_input), total_o, fin_o, fin_p, fin_q)
    return d_input, d_query.T, g_key.T, g_value.T


def solution(mesh):
    fine = Mesh(mesh.devices.reshape(4, 2, 4, 2, 2), ("x", "l", "z", "h", "c"))
    dp, tensor = ("x", "l"), ("z", "h", "c")
    return jax.shard_map(
        body,
        mesh=fine,
        in_specs=(P(dp + tensor, None), P(dp, tensor), P(dp, tensor), P(None, tensor), P(None, tensor)),
        out_specs=(P(dp + tensor, None), P(dp, tensor), P(dp, tensor), P(dp, tensor)),
        check_vma=False,
    )
```
